32 devices in a mesh: src: 2 (over x), space: 16 (over z, y, core).
Axes of the slice: x: 2, y: 2, z: 4, core: 2. Of those that a mesh axis runs over, the one named last changes fastest.
Arguments:
- fwd_current: float32 [2, 3, 128, 64, 128], P('src', None, 'space'), may hold values from -6 to 6
- adj_current: float32 [2, 3, 128, 64, 128], P('src', None, 'space'), may hold values from -6 to 6
- inv_eps: float32 [128, 64, 128], P('space'), may hold values from 0.25 to 1
- wavelength: int32 [2], P('src'), may hold values from 0 to 15
- footprint: int32 [128, 64], P('space', 'src'), may hold values from 0 to 511, as said below
Outputs:
- design_grad: float32 [512, 128], P(('src', 'space'))
The draws below stay inside these ranges and needn't reach their ends.
Inputs may be any that keep to these rules, and one draw needn't show every extreme that they name: `footprint`: A column (x, y) whose y lies in the i-th block of 32 cells names a pixel of the pixel blocks i * 16 to (i + 1) * 16 - 1, a pixel block being 16 consecutive pixels. Among the 256 columns of one slab of 8 cells in x and one block in y, at most 32 name pixels of any one pixel block; in each group i one pixel block receives exactly 32 columns from every slab.
All inputs are finite; a program needn't handle non-finite values.
Results may differ from the reference program's by a relative error of at most 0.0003.
Values sent between devices are 32-bit elements; how exact they have to be, the bound alone decides.
A program may use at most 64 MiB of HBM per device.

```python
import math
import jax
import jax.numpy as jnp
from jax import lax

CX = 8
NY = 64
NZ = 128
ITERS = 4
PIX_DEV = 16
NX = 128
SOURCES = 2
GROUPS = 2
OWNERS = 16
YSHARE = 32
ROWS = 256
CAP = 32
PIX = 512


def draw_footprint(key, part):
    slots = OWNERS * CAP
    heavy = jax.random.randint(jax.random.fold_in(key, 1), (GROUPS,), 0, OWNERS)

    def one_block(block_key, group):
        first, second, third = jax.random.split(block_key, 3)
        shuffled = jax.random.permutation(first, slots)
        owner = shuffled // CAP
        score = jnp.where(owner == heavy[group], 0, 1) * slots + jnp.arange(slots)
        order = jnp.argsort(score)
        chosen = shuffled[order][:ROWS]
        chosen = chosen[jax.random.permutation(second, ROWS)]
        within = jax.random.randint(third, (ROWS,), 0, PIX_DEV)
        return ((group * OWNERS + chosen // CAP) * PIX_DEV + within).astype(jnp.int32)
    block_keys = jax.random.split(jax.random.fold_in(key, 2), OWNERS * GROUPS)
    group_ids = jnp.tile(jnp.arange(GROUPS), OWNERS)
    pixels = jax.vmap(one_block)(block_keys, group_ids)
    pixels = pixels.reshape(OWNERS, GROUPS, CX, YSHARE).transpose(0, 2, 1, 3)
    return pixels.reshape(NX, NY).astype(jnp.int32)


def block_levels(own_key, shape, pieces, smallest, largest):
    loudness, own = 1.0, jax.random.fold_in(own_key, 6)
    for dim, blocks in pieces:
        steps = jnp.exp(jax.random.uniform(jax.random.fold_in(own, dim), (blocks,), jnp.float32, smallest / len(pieces), largest / len(pieces)))
        loudness = loudness * jnp.repeat(steps, shape[dim] // blocks).reshape([-1 if axis == dim else 1 for axis in range(len(shape))])
    return loudness


def bell_draw(key, dims, width, limit, pieces=(), kind=jnp.bfloat16):
    array = jax.random.normal(key, dims, jnp.float32) * width
    if len(pieces) > 0:
        array = block_levels(key, dims, pieces, -0.22, 0.18) * array
    return jnp.clip(array, min=-limit, max=limit).astype(kind)


def setup_inputs(seed: int = 0) -> dict:
    key_list = jax.random.split(jax.random.key(seed), 6)
    return {
        "fwd_current": bell_draw(key_list[0], (SOURCES, 3, NX, NY, NZ), 1.0, 6.0, ((0, 2), (2, 16)), jnp.float32),
        "adj_current": bell_draw(key_list[1], (SOURCES, 3, NX, NY, NZ), 1.0, 6.0, ((0, 2), (2, 16)), jnp.float32),
        "inv_eps": jnp.clip(jnp.exp(math.log(1.0) - 1.3862944 * jax.random.uniform(key_list[2], (NX, NY, NZ), jnp.float32) ** block_levels(key_list[2], (NX, NY, NZ), ((0, 16),), -0.2, 0.2)), 0.25, 1.0),
        "wavelength": jax.random.randint(key_list[3], (SOURCES,), 0, 16).astype(jnp.int32),
        "footprint": draw_footprint(jax.random.fold_in(key_list[5], 71), 0),
    }


COURANT = 0.5


def diff_fwd(field, axis):
    if axis == 0:
        ahead = jnp.concatenate([field[1:], jnp.zeros_like(field[:1])], axis=0)
    else:
        ahead = jnp.roll(field, -1, axis)
    return ahead - field


def diff_back(field, axis):
    if axis == 0:
        behind = jnp.concatenate([jnp.zeros_like(field[:1]), field[:-1]], axis=0)
    else:
        behind = jnp.roll(field, 1, axis)
    return field - behind


def curl_with(parts, differ):
    return (differ(parts[2], 1) - differ(parts[1], 2),
            differ(parts[0], 2) - differ(parts[2], 0),
            differ(parts[1], 0) - differ(parts[0], 1))


def evolve(current, omega, inv_eps, use_cos):
    zero = jnp.zeros(current.shape[1:], jnp.float32)
    electric = (zero, zero, zero)
    magnetic = (zero, zero, zero)
    stored = []
    for step in range(ITERS):
        phase = omega * (step + 1.0)
        signal = jnp.cos(phase) if use_cos else jnp.sin(phase)
        curl_e = curl_with(electric, diff_fwd)
        magnetic = tuple(magnetic[k] - COURANT * curl_e[k] for k in range(3))
        curl_h = curl_with(magnetic, diff_back)
        electric = tuple(electric[k] + COURANT * inv_eps * (curl_h[k] - current[k] * signal) for k in range(3))
        stored.append(electric)
    return stored


def reference(fwd_current, adj_current, inv_eps, wavelength, footprint):
    omegas = 0.25 + 0.05 * wavelength.astype(jnp.float32)

    def one_source(total, index):
        omega = omegas[index]
        forward = evolve(fwd_current[index], omega, inv_eps, False)
        adjoint = evolve(adj_current[index], omega, inv_eps, True)
        for step in range(ITERS):
            for k in range(3):
                total = total + forward[step][k] * adjoint[ITERS - 1 - step][k]
        return total, None

    start = jnp.zeros(inv_eps.shape, jnp.float32)
    grad, _ = lax.scan(one_source, start, jnp.arange(SOURCES, dtype=jnp.int32))
    flat = grad.reshape(NX * NY, NZ)
    return jax.ops.segment_sum(flat, footprint.reshape(NX * NY).astype(jnp.int32), num_segments=PIX)
```

```python
import functools

import jax
import jax.numpy as jnp
from jax import lax
from jax.experimental import pallas as pl
from jax.experimental.pallas import tpu as pltpu
from jax.sharding import PartitionSpec as P

ITERS = 4
PIX_DEV = 16
PIECES = ((3, 2), (0, 3), (5, 3))
MESH = pl.DeviceIdType.MESH


def ahead(f, axis):
    return pltpu.roll(f, f.shape[axis] - 1, axis)


def behind(f, axis):
    return pltpu.roll(f, 1, axis)


def next_h(h, e, e_next):
    e1, e2, e3 = e
    x2 = -e2 if e_next is None else e_next[0] - e2
    x3 = -e3 if e_next is None else e_next[1] - e3
    curl = (
        (ahead(e3, 0) - e3) - (ahead(e2, 1) - e2),
        (ahead(e1, 1) - e1) - x3,
        x2 - (ahead(e1, 0) - e1),
    )
    if h is None:
        return tuple(-v for v in curl)
    return tuple(a - v for a, v in zip(h, curl))


def curl_h(h, h_prev):
    h1, h2, h3 = h
    x2 = h2 if h_prev is None else h2 - h_prev[0]
    x3 = h3 if h_prev is None else h3 - h_prev[1]
    return (
        (h3 - behind(h3, 0)) - (h2 - behind(h2, 1)),
        (h1 - behind(h1, 1)) - x3,
        x2 - (h1 - behind(h1, 0)),
    )


def kernel(n, nsrc, fwd, adj, eps, wave, foot, out,
           J, C, E, H, HI, EL, EH, send_e, send_h, recv_e, recv_h, c_lo, c_hi,
           lo_h, lo_e, hi_e, sig, G, R, T, RT,
           load_sem, es_sem, er_sem, hs_sem, hr_sem, gs_sem, gr_sem, ts_sem, tr_sem):
    me = lax.axis_index("space")
    src = lax.axis_index("src")
    low, high = lax.rem(me + n - 1, n), lax.rem(me + 1, n)
    has_low, has_high = me > 0, me < n - 1
    ys = G.shape[2]

    loads = [
        pltpu.make_async_copy(eps, C, load_sem.at[0]),
        pltpu.make_async_copy(fwd.at[0], J.at[0], load_sem.at[1]),
        pltpu.make_async_copy(adj.at[0], J.at[1], load_sem.at[2]),
    ]
    for copy in loads:
        copy.start()

    barrier = pltpu.get_barrier_semaphore()
    for d in range(1, n):
        pl.semaphore_signal(barrier, inc=1, device_id={"space": lax.rem(me + d, n)}, device_id_type=MESH)
    for d in range(1, nsrc):
        pl.semaphore_signal(barrier, inc=1, device_id={"src": lax.rem(src + d, nsrc)}, device_id_type=MESH)

    omega = 0.25 + 0.05 * wave[0].astype(jnp.float32)
    when = (lax.broadcasted_iota(jnp.int32, (8, 128), 0) + 1).astype(jnp.float32)
    sig[0] = jnp.sin(omega * when)
    sig[1] = jnp.cos(omega * when)

    def remote(a, b, s, r, where):
        return pltpu.make_async_remote_copy(
            src_ref=a, dst_ref=b, send_sem=s, recv_sem=r, device_id=where, device_id_type=MESH)

    e_copies = [remote(send_e.at[t], recv_e.at[t], es_sem.at[t], er_sem.at[t], {"space": low}) for t in range(3)]
    e_copies.append(remote(eps.at[0], c_hi, es_sem.at[3], er_sem.at[3], {"space": low}))
    h_copies = [remote(send_h.at[t], recv_h.at[t], hs_sem.at[t], hr_sem.at[t], {"space": high}) for t in range(3)]
    h_copies.append(remote(eps.at[7], c_lo, hs_sem.at[3], hr_sem.at[3], {"space": high}))

    def start_e(t):
        pl.when(has_low)(lambda: e_copies[t].start())

    def start_h(t):
        pl.when(has_high)(lambda: h_copies[t].start())

    def arrived(t):
        pl.when(has_low)(lambda: h_copies[t].wait_recv())
        pl.when(has_high)(lambda: e_copies[t].wait_recv())

    @pl.when(jnp.logical_not(has_low))
    def _():
        recv_h[...] = jnp.zeros_like(recv_h)
        c_lo[...] = jnp.zeros_like(c_lo)

    @pl.when(jnp.logical_not(has_high))
    def _():
        recv_e[...] = jnp.zeros_like(recv_e)
        c_hi[...] = jnp.zeros_like(c_hi)

    m_lo = jnp.where(has_low, 1.0, 0.0).astype(jnp.float32)
    m_hi = jnp.where(has_high, 1.0, 0.0).astype(jnp.float32)

    def get(ref, *at):
        return tuple(ref[(*at[:-1], k, at[-1])] for k in range(3))

    def put(ref, vals, *at):
        for k in range(3):
            ref[(*at[:-1], k, at[-1])] = vals[k]

    def get3(ref, r):
        return tuple(ref[r, k] for k in range(3))

    def put3(ref, r, vals):
        for k in range(3):
            ref[r, k] = vals[k]

    def pair(ref, t, r):
        return ref[t, r, 0], ref[t, r, 1]

    def put_pair(ref, t, r, vals):
        ref[t, r, 0], ref[t, r, 1] = vals[1], vals[2]

    def e_at(t, r, p):
        return tuple(E[t, r, k, p] for k in range(3))

    def step_e(t, r, p, e, h, h_prev):
        c, s = C[p], sig[r, t:t + 1, :]
        curl = curl_h(h, h_prev)
        return tuple(e[k] + c * curl[k] - s * J[r, k, p] for k in range(3))

    def do_h(t, r, p):
        e, nxt = e_at(t, r, p), (E[t, r, 1, p + 1], E[t, r, 2, p + 1])
        put(H, next_h(None if t == 0 else get(H, r, p), e, nxt), r, p)

    def do_e(t, r, p):
        new = step_e(t, r, p, e_at(t - 1, r, p), get(H, r, p), (H[r, 1, p - 1], H[r, 2, p - 1]))
        for k in range(3):
            E[t, r, k, p] = new[k]

    def put_e(t, r, p, new):
        for k in range(3):
            E[t, r, k, p] = new[k]

    def runs(body):
        lax.fori_loop(0, 2, lambda r, _: (body(r), 0)[1], 0)

    def planes(first, last, body):
        count = last - first

        def one(i, _):
            body(i // count, first + i % count)
            return 0

        lax.fori_loop(0, 2 * count, one, 0)

    def begin(r, p):
        c2, s = 2.0 * C[p], sig[r, 0:1, :]
        for k in range(3):
            a = c2 * J[r, k, p]
            J[r, k, p] = a
            E[0, r, k, p] = -s * a

    pl.semaphore_wait(barrier, n - 1 + nsrc - 1)
    start_e(3)
    start_h(3)
    for copy in loads:
        copy.wait()

    def scale(p, _):
        C[p] = 0.25 * C[p]
        return 0

    lax.fori_loop(0, 8, scale, 0)

    def first(r):
        begin(r, 0)
        put_pair(send_e, 0, r, e_at(0, r, 0))
        begin(r, 7)
        h = next_h(None, e_at(0, r, 7), None)
        put3(HI, r, h)
        put_pair(send_h, 0, r, h)

    runs(first)
    start_e(0)
    start_h(0)
    planes(1, 7, begin)
    planes(0, 7, functools.partial(do_h, 0))

    def second(r):
        e = step_e(1, r, 0, e_at(0, r, 0), get(H, r, 0), None)
        put3(EL, r, e)
        put_pair(send_e, 1, r, e)

    runs(second)
    start_e(1)

    def third(r):
        do_e(1, r, 6)
        h7 = get3(HI, r)
        e7 = step_e(1, r, 7, e_at(0, r, 7), h7, (H[r, 1, 6], H[r, 2, 6]))
        put3(EH, r, e7)
        h7 = next_h(h7, e7, None)
        put3(HI, r, h7)
        put_pair(send_h, 1, r, h7)

    runs(third)
    start_h(1)

    def fourth(r):
        do_e(1, r, 1)
        e = get3(EL, r)
        h = next_h(get(H, r, 0), e, (E[1, r, 1, 1], E[1, r, 2, 1]))
        put_pair(send_e, 2, r, step_e(2, r, 0, e, h, None))

    runs(fourth)
    start_e(2)

    def fifth(r):
        e7, h7 = get3(EH, r), get3(HI, r)
        h6 = next_h(get(H, r, 6), e_at(1, r, 6), (e7[1], e7[2]))
        e7 = step_e(2, r, 7, e7, h7, (h6[1], h6[2]))
        put_pair(send_h, 2, r, next_h(h7, e7, None))

    runs(fifth)
    start_h(2)

    planes(2, 6, functools.partial(do_e, 1))
    planes(1, 6, functools.partial(do_h, 1))
    planes(2, 6, functools.partial(do_e, 2))
    planes(2, 5, functools.partial(do_h, 2))
    planes(3, 5, functools.partial(do_e, 3))

    def product(p):
        total = None
        for t in range(ITERS):
            for k in range(3):
                term = E[t, 0, k, p] * E[ITERS - 1 - t, 1, k, p]
                total = term if total is None else total + term
        for j in range(nsrc):
            G[j, p] = total[j * ys:(j + 1) * ys]

    def products(a, b):
        lax.fori_loop(a, b, lambda p, _: (product(p), 0)[1], 0)

    g_copies = []
    for piece, (start, size) in enumerate(PIECES):
        g_copies.append([
            remote(G.at[lax.rem(src + d, nsrc), pl.ds(start, size)], R.at[d - 1, pl.ds(start, size)],
                   gs_sem.at[d - 1, piece], gr_sem.at[d - 1, piece], {"src": lax.rem(src + d, nsrc)})
            for d in range(1, nsrc)
        ])

    def start_g(piece):
        for copy in g_copies[piece]:
            copy.start()

    products(3, 5)
    start_g(0)

    arrived(3)
    arrived(0)

    def step2(r):
        e0 = e_at(0, r, 0)
        d2, d3 = m_lo * e0[2], -m_lo * e0[1]
        zero = jnp.zeros_like(d2)
        h = pair(recv_h, 0, r)
        put_e(1, r, 0, step_e(1, r, 0, e0, get(H, r, 0), (h[0] + d2, h[1] + d3)))
        put3(lo_h, r, (zero, d2, d3))
        c = 0.25 * c_lo[...]
        put3(lo_e, r, tuple(c * v for v in curl_h((zero, d2, d3), None)))
        e7 = e_at(0, r, 7)
        h7 = next_h(None, e7, pair(recv_e, 0, r))
        put(H, h7, r, 7)
        put_e(1, r, 7, step_e(1, r, 7, e7, h7, (H[r, 1, 6], H[r, 2, 6])))
        c = m_hi * 0.25 * c_hi[...]
        put3(hi_e, r, (zero, c * h7[2], -c * h7[1]))

    runs(step2)
    arrived(1)

    def step3(r):
        do_h(1, r, 0)
        e0 = e_at(1, r, 0)
        de = get3(lo_e, r)
        dh = next_h(get3(lo_h, r), de, (m_lo * e0[1], m_lo * e0[2]))
        put3(lo_h, r, dh)
        h = pair(recv_h, 1, r)
        put_e(2, r, 0, step_e(2, r, 0, e0, get(H, r, 0), (h[0] + dh[1], h[1] + dh[2])))
        c = 0.25 * c_lo[...]
        curl = curl_h(dh, (de[2], -de[1]))
        put3(lo_e, r, tuple(de[k] + c * curl[k] for k in range(3)))
        do_e(2, r, 1)
        do_h(1, r, 6)
        de = get3(hi_e, r)
        e = pair(recv_e, 1, r)
        h7 = next_h(get(H, r, 7), e_at(1, r, 7), (e[0] + de[1], e[1] + de[2]))
        put(H, h7, r, 7)
        do_e(2, r, 7)
        do_e(2, r, 6)
        c = 0.25 * c_hi[...]
        curl = curl_h(next_h(None, de, None), (m_hi * h7[1], m_hi * h7[2]))
        put3(hi_e, r, tuple(de[k] + c * curl[k] for k in range(3)))

    runs(step3)
    arrived(2)

    def low4(r):
        e0 = e_at(2, r, 0)
        dh = next_h(get3(lo_h, r), get3(lo_e, r), (m_lo * e0[1], m_lo * e0[2]))
        h = pair(recv_h, 2, r)
        do_h(2, r, 0)
        do_h(2, r, 1)
        put_e(3, r, 0, step_e(3, r, 0, e0, get(H, r, 0), (h[0] + dh[1], h[1] + dh[2])))
        do_e(3, r, 1)
        do_e(3, r, 2)

    runs(low4)
    products(0, 3)
    start_g(1)

    def high4(r):
        de = get3(hi_e, r)
        e = pair(recv_e, 2, r)
        put(H, next_h(get(H, r, 7), e_at(2, r, 7), (e[0] + de[1], e[1] + de[2])), r, 7)
        do_h(2, r, 6)
        do_h(2, r, 5)
        do_e(3, r, 7)
        do_e(3, r, 6)
        do_e(3, r, 5)

    runs(high4)
    products(5, 8)
    start_g(2)

    pixels = n * PIX_DEV
    ids = foot[...] - src * pixels
    row = lax.broadcasted_iota(jnp.int32, (pixels, ys), 0)
    chosen = [(row == ids[p:p + 1, :]).astype(jnp.float32).astype(jnp.bfloat16) for p in range(8)]
    total = jnp.zeros((pixels, 128), jnp.float32)
    for piece, (start, size) in enumerate(PIECES):
        for copy in g_copies[piece]:
            copy.wait_recv()
        for p in range(start, start + size):
            block = G[src, p]
            for d in range(1, nsrc):
                block = block + R[d - 1, p]
            head = block.astype(jnp.bfloat16)
            tail = (block - head.astype(jnp.float32)).astype(jnp.bfloat16)
            total = total + jnp.dot(chosen[p], head, preferred_element_type=jnp.float32)
            total = total + jnp.dot(chosen[p], tail, preferred_element_type=jnp.float32)
    T[...] = total.reshape(n, PIX_DEV, 128)

    t_copies = [
        remote(T.at[lax.rem(me + d, n)], RT.at[d - 1], ts_sem.at[d - 1], tr_sem.at[d - 1],
               {"space": lax.rem(me + d, n)})
        for d in range(1, n)
    ]
    for copy in t_copies:
        copy.start()
    result = T[me]
    for d in range(1, n):
        t_copies[d - 1].wait_recv()
        result = result + RT[d - 1]
    out[...] = result

    for copy in t_copies:
        copy.wait_send()
    for piece in g_copies:
        for copy in piece:
            copy.wait_send()
    for t in range(4):
        pl.when(has_low)(lambda: e_copies[t].wait_send())
        pl.when(has_high)(lambda: h_copies[t].wait_send())


def solution(mesh):
    n, nsrc = mesh.shape["space"], mesh.shape["src"]

    def per_device(fwd, adj, eps, wave, foot):
        cx, ny, nz = eps.shape
        ys = foot.shape[1]
        f32 = jnp.float32
        plane = (ny, nz)

        def vmem(*shape):
            return pltpu.VMEM(shape, f32)

        dma = pltpu.SemaphoreType.DMA
        any_spec = pl.BlockSpec(memory_space=pl.ANY)
        return pl.pallas_call(
            functools.partial(kernel, n, nsrc),
            out_shape=jax.ShapeDtypeStruct((PIX_DEV, nz), f32),
            in_specs=[any_spec, any_spec, any_spec, pl.BlockSpec(memory_space=pltpu.SMEM),
                      pl.BlockSpec(memory_space=pltpu.VMEM)],
            out_specs=pl.BlockSpec(memory_space=pltpu.VMEM),
            scratch_shapes=[
                vmem(2, 3, cx, *plane), vmem(cx, *plane), vmem(ITERS, 2, 3, cx, *plane),
                vmem(2, 3, cx, *plane), vmem(2, 3, *plane), vmem(2, 3, *plane), vmem(2, 3, *plane),
                vmem(3, 2, 2, *plane), vmem(3, 2, 2, *plane), vmem(3, 2, 2, *plane), vmem(3, 2, 2, *plane),
                vmem(*plane), vmem(*plane),
                vmem(2, 3, *plane), vmem(2, 3, *plane), vmem(2, 3, *plane), vmem(2, 8, 128),
                vmem(nsrc, cx, ys, nz), vmem(nsrc - 1, cx, ys, nz),
                vmem(n, PIX_DEV, nz), vmem(n - 1, PIX_DEV, nz),
                dma((3,)), dma((4,)), dma((4,)), dma((4,)), dma((4,)),
                dma((nsrc - 1, 3)), dma((nsrc - 1, 3)), dma((n - 1,)), dma((n - 1,)),
            ],
            compiler_params=pltpu.CompilerParams(
                collective_id=0, has_side_effects=True, vmem_limit_bytes=40 * 1024 * 1024),
            cost_estimate=pl.CostEstimate(flops=30_000_000, bytes_accessed=2_000_000, transcendentals=0),
        )(fwd, adj, eps, wave, foot)

    in_specs = (
        P("src", None, "space", None, None),
        P("src", None, "space", None, None),
        P("space", None, None),
        P("src"),
        P("space", "src"),
    )
    return jax.shard_map(
        per_device, mesh=mesh, in_specs=in_specs, out_specs=P(("src", "space"), None), check_vma=False)
```

```python
import functools

import jax
import jax.numpy as jnp
from jax import lax
from jax.experimental import pallas as pl
from jax.experimental.pallas import tpu as pltpu
from jax.sharding import PartitionSpec as P

ITERS = 4
PIX_DEV = 16
PIECES = ((3, 2), (0, 3), (5, 3))
MESH = pl.DeviceIdType.MESH


def ahead(f, axis):
    if axis == 1:
        return pltpu.roll(f, f.shape[2] - 1, 2)
    return jnp.concatenate([f[1:], pltpu.roll(f[:1], 7, 1)], axis=0)


def behind(f, axis):
    if axis == 1:
        return pltpu.roll(f, 1, 2)
    return jnp.concatenate([pltpu.roll(f[-1:], 1, 1), f[:-1]], axis=0)


def dealt(ref, *at):
    folds = ref.shape[-2] // 8
    return jnp.stack([ref[(*at, pl.ds(j, 8, stride=folds), slice(None))] for j in range(folds)])


def next_h(h, e, e_next):
    e1, e2, e3 = e
    x2 = -e2 if e_next is None else e_next[0] - e2
    x3 = -e3 if e_next is None else e_next[1] - e3
    curl = (
        (ahead(e3, 0) - e3) - (ahead(e2, 1) - e2),
        (ahead(e1, 1) - e1) - x3,
        x2 - (ahead(e1, 0) - e1),
    )
    if h is None:
        return tuple(-v for v in curl)
    return tuple(a - v for a, v in zip(h, curl))


def curl_h(h, h_prev):
    h1, h2, h3 = h
    x2 = h2 if h_prev is None else h2 - h_prev[0]
    x3 = h3 if h_prev is None else h3 - h_prev[1]
    return (
        (h3 - behind(h3, 0)) - (h2 - behind(h2, 1)),
        (h1 - behind(h1, 1)) - x3,
        x2 - (h1 - behind(h1, 0)),
    )


def kernel(n, nsrc, fwd, adj, eps, wave, foot_hbm, out,
           foot, JR, CR, J, C, E, H, HI, EL, EH, send_e, send_h, recv_e, recv_h, c_lo, c_hi,
           lo_h, lo_e, hi_e, sig, G, R, T, RT,
           load_sem, es_sem, er_sem, hs_sem, hr_sem, gs_sem, gr_sem, ts_sem, tr_sem):
    me = lax.axis_index("space")
    src = lax.axis_index("src")
    low, high = lax.rem(me + n - 1, n), lax.rem(me + 1, n)
    has_low, has_high = me > 0, me < n - 1
    ys = foot.shape[1]

    loads = [
        pltpu.make_async_copy(eps, CR, load_sem.at[0]),
        pltpu.make_async_copy(fwd.at[0], JR.at[0], load_sem.at[1]),
        pltpu.make_async_copy(adj.at[0], JR.at[1], load_sem.at[2]),
        pltpu.make_async_copy(foot_hbm, foot, load_sem.at[3]),
    ]
    for copy in loads:
        copy.start()

    barrier = pltpu.get_barrier_semaphore()
    for d in range(1, n):
        pl.semaphore_signal(barrier, inc=1, device_id={"space": lax.rem(me + d, n)}, device_id_type=MESH)
    for d in range(1, nsrc):
        pl.semaphore_signal(barrier, inc=1, device_id={"src": lax.rem(src + d, nsrc)}, device_id_type=MESH)

    omega = 0.25 + 0.05 * wave[0].astype(jnp.float32)
    when = (lax.broadcasted_iota(jnp.int32, (8, 128), 0) + 1).astype(jnp.float32)
    sig[0] = jnp.sin(omega * when)
    sig[1] = jnp.cos(omega * when)

    def remote(a, b, s, r, where):
        return pltpu.make_async_remote_copy(
            src_ref=a, dst_ref=b, send_sem=s, recv_sem=r, device_id=where, device_id_type=MESH)

    e_copies = [remote(send_e.at[t], recv_e.at[t], es_sem.at[t], er_sem.at[t], {"space": low}) for t in range(3)]
    e_copies.append(remote(eps.at[0], c_hi, es_sem.at[3], er_sem.at[3], {"space": low}))
    h_copies = [remote(send_h.at[t], recv_h.at[t], hs_sem.at[t], hr_sem.at[t], {"space": high}) for t in range(3)]
    h_copies.append(remote(eps.at[7], c_lo, hs_sem.at[3], hr_sem.at[3], {"space": high}))

    def start_e(t):
        pl.when(has_low)(lambda: e_copies[t].start())

    def start_h(t):
        pl.when(has_high)(lambda: h_copies[t].start())

    def arrived(t):
        pl.when(has_low)(lambda: h_copies[t].wait_recv())
        pl.when(has_high)(lambda: e_copies[t].wait_recv())

    @pl.when(jnp.logical_not(has_low))
    def _():
        recv_h[...] = jnp.zeros_like(recv_h)
        c_lo[...] = jnp.zeros_like(c_lo)

    @pl.when(jnp.logical_not(has_high))
    def _():
        recv_e[...] = jnp.zeros_like(recv_e)
        c_hi[...] = jnp.zeros_like(c_hi)

    m_lo = jnp.where(has_low, 1.0, 0.0).astype(jnp.float32)
    m_hi = jnp.where(has_high, 1.0, 0.0).astype(jnp.float32)

    def get(ref, *at):
        return tuple(ref[(*at[:-1], k, at[-1])] for k in range(3))

    def put(ref, vals, *at):
        for k in range(3):
            ref[(*at[:-1], k, at[-1])] = vals[k]

    def get3(ref, r):
        return tuple(ref[r, k] for k in range(3))

    def put3(ref, r, vals):
        for k in range(3):
            ref[r, k] = vals[k]

    def pair(ref, t, r):
        return ref[t, r, 0], ref[t, r, 1]

    def put_pair(ref, t, r, vals):
        ref[t, r, 0], ref[t, r, 1] = vals[1], vals[2]

    def e_at(t, r, p):
        return tuple(E[t, r, k, p] for k in range(3))

    def step_e(t, r, p, e, h, h_prev):
        c, s = C[p], sig[r, t:t + 1, :]
        curl = curl_h(h, h_prev)
        return tuple(e[k] + c * curl[k] - s * J[r, k, p] for k in range(3))

    def do_h(t, r, p):
        e, nxt = e_at(t, r, p), (E[t, r, 1, p + 1], E[t, r, 2, p + 1])
        put(H, next_h(None if t == 0 else get(H, r, p), e, nxt), r, p)

    def do_e(t, r, p):
        new = step_e(t, r, p, e_at(t - 1, r, p), get(H, r, p), (H[r, 1, p - 1], H[r, 2, p - 1]))
        for k in range(3):
            E[t, r, k, p] = new[k]

    def put_e(t, r, p, new):
        for k in range(3):
            E[t, r, k, p] = new[k]

    def runs(body):
        lax.fori_loop(0, 2, lambda r, _: (body(r), 0)[1], 0)

    def planes(first, last, body):
        def one(p, _):
            body(0, p)
            body(1, p)
            return 0

        lax.fori_loop(first, last, one, 0)

    def begin(r, p):
        c2, s = 2.0 * C[p], sig[r, 0:1, :]
        for k in range(3):
            a = c2 * dealt(JR, r, k, p)
            J[r, k, p] = a
            E[0, r, k, p] = -s * a

    for copy in loads:
        copy.wait()

    def scale(p, _):
        C[p] = 0.25 * dealt(CR, p)
        return 0

    lax.fori_loop(0, 8, scale, 0)

    def first(r):
        begin(r, 0)
        put_pair(send_e, 0, r, e_at(0, r, 0))
        begin(r, 7)
        h = next_h(None, e_at(0, r, 7), None)
        put3(HI, r, h)
        put_pair(send_h, 0, r, h)

    runs(first)
    pl.semaphore_wait(barrier, n - 1 + nsrc - 1)
    start_e(3)
    start_h(3)
    start_e(0)
    start_h(0)
    planes(1, 7, begin)
    planes(0, 7, functools.partial(do_h, 0))

    def second(r):
        e = step_e(1, r, 0, e_at(0, r, 0), get(H, r, 0), None)
        put3(EL, r, e)
        put_pair(send_e, 1, r, e)

    runs(second)
    start_e(1)

    def third(r):
        do_e(1, r, 6)
        h7 = get3(HI, r)
        e7 = step_e(1, r, 7, e_at(0, r, 7), h7, (H[r, 1, 6], H[r, 2, 6]))
        put3(EH, r, e7)
        h7 = next_h(h7, e7, None)
        put3(HI, r, h7)
        put_pair(send_h, 1, r, h7)

    runs(third)
    start_h(1)

    def fourth(r):
        do_e(1, r, 1)
        e = get3(EL, r)
        h = next_h(get(H, r, 0), e, (E[1, r, 1, 1], E[1, r, 2, 1]))
        put_pair(send_e, 2, r, step_e(2, r, 0, e, h, None))

    runs(fourth)
    start_e(2)

    def fifth(r):
        e7, h7 = get3(EH, r), get3(HI, r)
        h6 = next_h(get(H, r, 6), e_at(1, r, 6), (e7[1], e7[2]))
        e7 = step_e(2, r, 7, e7, h7, (h6[1], h6[2]))
        put_pair(send_h, 2, r, next_h(h7, e7, None))

    runs(fifth)
    start_h(2)

    planes(2, 6, functools.partial(do_e, 1))
    planes(1, 6, functools.partial(do_h, 1))
    planes(2, 6, functools.partial(do_e, 2))
    planes(2, 5, functools.partial(do_h, 2))
    planes(3, 5, functools.partial(do_e, 3))

    def product(p):
        total = None
        for t in range(ITERS):
            for k in range(3):
                term = E[t, 0, k, p] * E[ITERS - 1 - t, 1, k, p]
                total = term if total is None else total + term
        folds = total.shape[0]
        for j in range(folds):
            G[p, pl.ds(j, 8, stride=folds), :] = total[j]

    def products(a, b):
        lax.fori_loop(a, b, lambda p, _: (product(p), 0)[1], 0)

    def share(j):
        return pl.ds(pl.multiple_of(j * ys, 8), ys)

    g_copies = []
    for piece, (start, size) in enumerate(PIECES):
        g_copies.append([
            remote(G.at[pl.ds(start, size), share(lax.rem(src + d, nsrc))], R.at[d - 1, pl.ds(start, size)],
                   gs_sem.at[d - 1, piece], gr_sem.at[d - 1, piece], {"src": lax.rem(src + d, nsrc)})
            for d in range(1, nsrc)
        ])

    def start_g(piece):
        for copy in g_copies[piece]:
            copy.start()

    products(3, 5)
    start_g(0)

    arrived(3)
    arrived(0)

    def step2(r):
        e0 = e_at(0, r, 0)
        d2, d3 = m_lo * e0[2], -m_lo * e0[1]
        zero = jnp.zeros_like(d2)
        h = pair(recv_h, 0, r)
        put_e(1, r, 0, step_e(1, r, 0, e0, get(H, r, 0), (h[0] + d2, h[1] + d3)))
        put3(lo_h, r, (zero, d2, d3))
        c = 0.25 * dealt(c_lo)
        put3(lo_e, r, tuple(c * v for v in curl_h((zero, d2, d3), None)))
        e7 = e_at(0, r, 7)
        h7 = next_h(None, e7, pair(recv_e, 0, r))
        put(H, h7, r, 7)
        put_e(1, r, 7, step_e(1, r, 7, e7, h7, (H[r, 1, 6], H[r, 2, 6])))
        c = m_hi * 0.25 * dealt(c_hi)
        put3(hi_e, r, (zero, c * h7[2], -c * h7[1]))

    runs(step2)
    arrived(1)

    def step3(r):
        do_h(1, r, 0)
        e0 = e_at(1, r, 0)
        de = get3(lo_e, r)
        dh = next_h(get3(lo_h, r), de, (m_lo * e0[1], m_lo * e0[2]))
        put3(lo_h, r, dh)
        h = pair(recv_h, 1, r)
        put_e(2, r, 0, step_e(2, r, 0, e0, get(H, r, 0), (h[0] + dh[1], h[1] + dh[2])))
        c = 0.25 * dealt(c_lo)
        curl = curl_h(dh, (de[2], -de[1]))
        put3(lo_e, r, tuple(de[k] + c * curl[k] for k in range(3)))
        do_e(2, r, 1)
        do_h(1, r, 6)
        de = get3(hi_e, r)
        e = pair(recv_e, 1, r)
        h7 = next_h(get(H, r, 7), e_at(1, r, 7), (e[0] + de[1], e[1] + de[2]))
        put(H, h7, r, 7)
        do_e(2, r, 7)
        do_e(2, r, 6)
        c = 0.25 * dealt(c_hi)
        curl = curl_h(next_h(None, de, None), (m_hi * h7[1], m_hi * h7[2]))
        put3(hi_e, r, tuple(de[k] + c * curl[k] for k in range(3)))

    runs(step3)
    arrived(2)

    def low4(r):
        e0 = e_at(2, r, 0)
        dh = next_h(get3(lo_h, r), get3(lo_e, r), (m_lo * e0[1], m_lo * e0[2]))
        h = pair(recv_h, 2, r)
        do_h(2, r, 0)
        do_h(2, r, 1)
        put_e(3, r, 0, step_e(3, r, 0, e0, get(H, r, 0), (h[0] + dh[1], h[1] + dh[2])))
        do_e(3, r, 1)
        do_e(3, r, 2)

    runs(low4)
    products(0, 3)
    start_g(1)

    def high4(r):
        de = get3(hi_e, r)
        e = pair(recv_e, 2, r)
        put(H, next_h(get(H, r, 7), e_at(2, r, 7), (e[0] + de[1], e[1] + de[2])), r, 7)
        do_h(2, r, 6)
        do_h(2, r, 5)
        do_e(3, r, 7)
        do_e(3, r, 6)
        do_e(3, r, 5)

    runs(high4)
    products(5, 8)
    start_g(2)

    pixels = n * PIX_DEV
    ids = foot[...] - src * pixels
    row = lax.broadcasted_iota(jnp.int32, (pixels, ys), 0)
    chosen = [(row == ids[p:p + 1, :]).astype(jnp.float32).astype(jnp.bfloat16) for p in range(8)]
    total = jnp.zeros((pixels, 128), jnp.float32)
    for piece, (start, size) in enumerate(PIECES):
        for copy in g_copies[piece]:
            copy.wait_recv()
        for p in range(start, start + size):
            block = G[p, share(src), :]
            for d in range(1, nsrc):
                block = block + R[d - 1, p]
            head = block.astype(jnp.bfloat16)
            tail = (block - head.astype(jnp.float32)).astype(jnp.bfloat16)
            total = total + jnp.dot(chosen[p], head, preferred_element_type=jnp.float32)
            total = total + jnp.dot(chosen[p], tail, preferred_element_type=jnp.float32)
    T[...] = total.reshape(n, PIX_DEV, 128)

    t_copies = [
        remote(T.at[lax.rem(me + d, n)], RT.at[d - 1], ts_sem.at[d - 1], tr_sem.at[d - 1],
               {"space": lax.rem(me + d, n)})
        for d in range(1, n)
    ]
    for copy in t_copies:
        copy.start()
    result = T[me]
    for d in range(1, n):
        t_copies[d - 1].wait_recv()
        result = result + RT[d - 1]
    out[...] = result

    for copy in t_copies:
        copy.wait_send()
    for piece in g_copies:
        for copy in piece:
            copy.wait_send()
    for t in range(4):
        pl.when(has_low)(lambda: e_copies[t].wait_send())
        pl.when(has_high)(lambda: h_copies[t].wait_send())


def solution(mesh):
    n, nsrc = mesh.shape["space"], mesh.shape["src"]

    def per_device(fwd, adj, eps, wave, foot):
        cx, ny, nz = eps.shape
        ys = foot.shape[1]
        f32 = jnp.float32
        raw, plane = (ny, nz), (ny // 8, 8, nz)

        def vmem(*shape):
            return pltpu.VMEM(shape, f32)

        dma = pltpu.SemaphoreType.DMA
        hbm = pl.BlockSpec(memory_space=pltpu.HBM)
        return pl.pallas_call(
            functools.partial(kernel, n, nsrc),
            out_shape=jax.ShapeDtypeStruct((PIX_DEV, nz), f32),
            in_specs=[hbm, hbm, hbm, pl.BlockSpec(memory_space=pltpu.SMEM), hbm],
            out_specs=pl.BlockSpec(memory_space=pltpu.VMEM),
            scratch_shapes=[
                pltpu.VMEM(foot.shape, jnp.int32), vmem(2, 3, cx, *raw), vmem(cx, *raw),
                vmem(2, 3, cx, *plane), vmem(cx, *plane), vmem(ITERS, 2, 3, cx, *plane),
                vmem(2, 3, cx, *plane), vmem(2, 3, *plane), vmem(2, 3, *plane), vmem(2, 3, *plane),
                vmem(3, 2, 2, *plane), vmem(3, 2, 2, *plane), vmem(3, 2, 2, *plane), vmem(3, 2, 2, *plane),
                vmem(*raw), vmem(*raw),
                vmem(2, 3, *plane), vmem(2, 3, *plane), vmem(2, 3, *plane), vmem(2, 8, 128),
                vmem(cx, *raw), vmem(nsrc - 1, cx, ys, nz),
                vmem(n, PIX_DEV, nz), vmem(n - 1, PIX_DEV, nz),
                dma((4,)), dma((4,)), dma((4,)), dma((4,)), dma((4,)),
                dma((nsrc - 1, 3)), dma((nsrc - 1, 3)), dma((n - 1,)), dma((n - 1,)),
            ],
            compiler_params=pltpu.CompilerParams(
                collective_id=0, has_side_effects=True, vmem_limit_bytes=40 * 1024 * 1024),
            cost_estimate=pl.CostEstimate(flops=30_000_000, bytes_accessed=2_000_000, transcendentals=0),
        )(fwd, adj, eps, wave, foot)

    in_specs = (
        P("src", None, "space", None, None),
        P("src", None, "space", None, None),
        P("space", None, None),
        P("src"),
        P("space", "src"),
    )
    return jax.shard_map(
        per_device, mesh=mesh, in_specs=in_specs, out_specs=P(("src", "space"), None), check_vma=False)
```

```python
import functools

import jax
import jax.numpy as jnp
from jax import lax
from jax.experimental import pallas as pl
from jax.experimental.pallas import tpu as pltpu
from jax.sharding import PartitionSpec as P

ITERS = 4
PIX_DEV = 16
PIECES = ((2, 4), (1, 1), (6, 1), (0, 1), (7, 1))
MESH = pl.DeviceIdType.MESH


def ahead(f, axis):
    if axis == 1:
        return pltpu.roll(f, f.shape[2] - 1, 2)
    return jnp.concatenate([f[1:], pltpu.roll(f[:1], 7, 1)], axis=0)


def behind(f, axis):
    if axis == 1:
        return pltpu.roll(f, 1, 2)
    return jnp.concatenate([pltpu.roll(f[-1:], 1, 1), f[:-1]], axis=0)


def dealt(ref, *at):
    folds = ref.shape[-2] // 8
    return jnp.stack([ref[(*at, pl.ds(j, 8, stride=folds), slice(None))] for j in range(folds)])


def next_h(h, e, e_next):
    e1, e2, e3 = e
    x2 = -e2 if e_next is None else e_next[0] - e2
    x3 = -e3 if e_next is None else e_next[1] - e3
    curl = (
        (ahead(e3, 0) - e3) - (ahead(e2, 1) - e2),
        (ahead(e1, 1) - e1) - x3,
        x2 - (ahead(e1, 0) - e1),
    )
    if h is None:
        return tuple(-v for v in curl)
    return tuple(a - v for a, v in zip(h, curl))


def curl_h(h, h_prev):
    h1, h2, h3 = h
    x2 = h2 if h_prev is None else h2 - h_prev[0]
    x3 = h3 if h_prev is None else h3 - h_prev[1]
    return (
        (h3 - behind(h3, 0)) - (h2 - behind(h2, 1)),
        (h1 - behind(h1, 1)) - x3,
        x2 - (h1 - behind(h1, 0)),
    )


def kernel(n, nsrc, fwd, adj, eps, wave, foot_hbm, out,
           foot, JR, CR, J, C, E, H, HI, EL, EH, send_e, send_h, recv_e, recv_h, c_lo, c_hi, j_lo, j_hi,
           q_lo, q_hi, r_lo, r_hi, b_lo, b_hi, e_lo, e_hi, lo_h, lo_e, hi_e, sig, G, R, T, RT,
           load_sem, es_sem, er_sem, hs_sem, hr_sem, gs_sem, gr_sem, ts_sem, tr_sem):
    me = lax.axis_index("space")
    src = lax.axis_index("src")
    low, high = lax.rem(me + n - 1, n), lax.rem(me + 1, n)
    has_low, has_high = me > 0, me < n - 1
    ys = foot.shape[1]

    loads = [
        pltpu.make_async_copy(eps, CR, load_sem.at[0]),
        pltpu.make_async_copy(fwd.at[0], JR.at[0], load_sem.at[1]),
        pltpu.make_async_copy(adj.at[0], JR.at[1], load_sem.at[2]),
        pltpu.make_async_copy(foot_hbm, foot, load_sem.at[3]),
    ]
    for copy in loads:
        copy.start()

    barrier = pltpu.get_barrier_semaphore()
    for d in range(1, n):
        pl.semaphore_signal(barrier, inc=1, device_id={"space": lax.rem(me + d, n)}, device_id_type=MESH)
    for d in range(1, nsrc):
        pl.semaphore_signal(barrier, inc=1, device_id={"src": lax.rem(src + d, nsrc)}, device_id_type=MESH)

    omega = 0.25 + 0.05 * wave[0].astype(jnp.float32)
    when = (lax.broadcasted_iota(jnp.int32, (8, 128), 0) + 1).astype(jnp.float32)
    sig[0] = jnp.sin(omega * when)
    sig[1] = jnp.cos(omega * when)

    def remote(a, b, s, r, where):
        return pltpu.make_async_remote_copy(
            src_ref=a, dst_ref=b, send_sem=s, recv_sem=r, device_id=where, device_id_type=MESH)

    def copies(pairs, s, r, where):
        return [remote(a, b, s.at[i], r.at[i], where) for i, (a, b) in enumerate(pairs)]

    e_copies = copies((
        (fwd.at[0, pl.ds(1, 2), 0], j_hi.at[0]), (adj.at[0, pl.ds(1, 2), 0], j_hi.at[1]), (eps.at[0], c_hi),
        (send_e, recv_e), (q_lo, r_hi)), es_sem, er_sem, {"space": low})
    h_copies = copies((
        (fwd.at[0, :, 7], j_lo.at[0]), (adj.at[0, :, 7], j_lo.at[1]), (eps.at[7], c_lo),
        (send_h, recv_h), (q_hi, r_lo)), hs_sem, hr_sem, {"space": high})

    def start_e(*those):
        pl.when(has_low)(lambda: [e_copies[i].start() for i in those] and None)

    def start_h(*those):
        pl.when(has_high)(lambda: [h_copies[i].start() for i in those] and None)

    def arrived(*those):
        pl.when(has_low)(lambda: [h_copies[i].wait_recv() for i in those] and None)
        pl.when(has_high)(lambda: [e_copies[i].wait_recv() for i in those] and None)

    @pl.when(jnp.logical_not(has_low))
    def _():
        for ref in (recv_h, c_lo, j_lo, r_lo):
            ref[...] = jnp.zeros_like(ref)

    @pl.when(jnp.logical_not(has_high))
    def _():
        for ref in (recv_e, c_hi, j_hi, r_hi):
            ref[...] = jnp.zeros_like(ref)

    m_lo = jnp.where(has_low, 1.0, 0.0).astype(jnp.float32)
    m_hi = jnp.where(has_high, 1.0, 0.0).astype(jnp.float32)

    def get(ref, *at):
        return tuple(ref[(*at[:-1], k, at[-1])] for k in range(3))

    def put(ref, vals, *at):
        for k in range(3):
            ref[(*at[:-1], k, at[-1])] = vals[k]

    def get3(ref, r):
        return tuple(ref[r, k] for k in range(3))

    def put3(ref, r, vals):
        for k in range(3):
            ref[r, k] = vals[k]

    def pair(ref, r):
        return ref[r, 0], ref[r, 1]

    def put_pair(ref, r, vals):
        ref[r, 0], ref[r, 1] = vals[1], vals[2]

    def e_at(t, r, p):
        return tuple(E[t, r, k, p] for k in range(3))

    def step_e(t, r, p, e, h, h_prev):
        c, s = C[p], sig[r, t:t + 1, :]
        curl = curl_h(h, h_prev)
        return tuple(e[k] + c * curl[k] - s * J[r, k, p] for k in range(3))

    def do_h(t, r, p):
        e, nxt = e_at(t, r, p), (E[t, r, 1, p + 1], E[t, r, 2, p + 1])
        put(H, next_h(None if t == 0 else get(H, r, p), e, nxt), r, p)

    def do_e(t, r, p):
        new = step_e(t, r, p, e_at(t - 1, r, p), get(H, r, p), (H[r, 1, p - 1], H[r, 2, p - 1]))
        for k in range(3):
            E[t, r, k, p] = new[k]

    def put_e(t, r, p, new):
        for k in range(3):
            E[t, r, k, p] = new[k]

    def runs(body):
        lax.fori_loop(0, 2, lambda r, _: (body(r), 0)[1], 0)

    def planes(first, last, body):
        def one(p, _):
            body(0, p)
            body(1, p)
            return 0

        lax.fori_loop(first, last, one, 0)

    def begin(r, p):
        c2, s = 2.0 * C[p], sig[r, 0:1, :]
        for k in range(3):
            a = c2 * dealt(JR, r, k, p)
            J[r, k, p] = a
            E[0, r, k, p] = -s * a

    pl.semaphore_wait(barrier, n - 1 + nsrc - 1)
    start_e(0, 1, 2)
    start_h(0, 1, 2)
    for copy in loads:
        copy.wait()

    def scale(p, _):
        C[p] = 0.25 * dealt(CR, p)
        return 0

    lax.fori_loop(0, 8, scale, 0)
    planes(0, 8, begin)
    planes(0, 7, functools.partial(do_h, 0))

    def alone_low(r):
        e = step_e(1, r, 0, e_at(0, r, 0), get(H, r, 0), None)
        put3(EL, r, e)
        put_pair(send_e, r, e)

    runs(alone_low)
    start_e(3)

    def alone_high(r):
        do_e(1, r, 6)
        h7 = next_h(None, e_at(0, r, 7), None)
        e7 = step_e(1, r, 7, e_at(0, r, 7), h7, (H[r, 1, 6], H[r, 2, 6]))
        put3(EH, r, e7)
        h7 = next_h(h7, e7, None)
        put3(HI, r, h7)
        put_pair(send_h, r, h7)

    runs(alone_high)
    start_h(3)

    def alone_last(r):
        do_e(1, r, 1)
        e = get3(EL, r)
        h = next_h(get(H, r, 0), e, (E[1, r, 1, 1], E[1, r, 2, 1]))
        put3(EL, r, step_e(2, r, 0, e, h, None))
        e7, h7 = get3(EH, r), get3(HI, r)
        h6 = next_h(get(H, r, 6), e_at(1, r, 6), (e7[1], e7[2]))
        e7 = step_e(2, r, 7, e7, h7, (h6[1], h6[2]))
        put3(HI, r, next_h(h7, e7, None))

    runs(alone_last)

    planes(2, 6, functools.partial(do_e, 1))
    planes(1, 6, functools.partial(do_h, 1))
    planes(2, 6, functools.partial(do_e, 2))
    planes(2, 5, functools.partial(do_h, 2))
    planes(3, 5, functools.partial(do_e, 3))

    arrived(0, 1, 2)
    b_lo[...] = 0.25 * dealt(c_lo)
    b_hi[...] = 0.25 * dealt(c_hi)

    def edges(r):
        s = sig[r, 0:1, :]
        for k in range(3):
            e_lo[r, k] = -s * (2.0 * b_lo[...] * dealt(j_lo, r, k))
        for k in range(2):
            e_hi[r, k] = -s * (2.0 * b_hi[...] * dealt(j_hi, r, k))

    runs(edges)
    for_low, for_high = None, None
    for r in range(2):
        curl = curl_h((jnp.zeros_like(EL[r, 0]), EL[r, 2], -EL[r, 1]), None)
        terms = [e_lo[1 - r, k] * curl[k] for k in range(3)]
        term = terms[0] + terms[1] + terms[2]
        for_low = term if for_low is None else for_low + term
        term = e_hi[1 - r, 0] * HI[r, 2] - e_hi[1 - r, 1] * HI[r, 1]
        for_high = term if for_high is None else for_high + term
    q_lo[...] = b_lo[...] * for_low
    q_hi[...] = b_hi[...] * for_high
    start_e(4)
    start_h(4)

    def product(p, more=None):
        total = more
        for t in range(ITERS):
            for k in range(3):
                term = E[t, 0, k, p] * E[ITERS - 1 - t, 1, k, p]
                total = term if total is None else total + term
        folds = total.shape[0]
        for j in range(folds):
            G[p, pl.ds(j, 8, stride=folds), :] = total[j]

    def share(j):
        return pl.ds(pl.multiple_of(j * ys, 8), ys)

    g_copies = []
    for piece, (start, size) in enumerate(PIECES):
        g_copies.append([
            remote(G.at[pl.ds(start, size), share(lax.rem(src + d, nsrc))], R.at[d - 1, pl.ds(start, size)],
                   gs_sem.at[d - 1, piece], gr_sem.at[d - 1, piece], {"src": lax.rem(src + d, nsrc)})
            for d in range(1, nsrc)
        ])

    def start_g(piece):
        for copy in g_copies[piece]:
            copy.start()

    def step2(r):
        e0 = e_at(0, r, 0)
        d2, d3 = m_lo * e0[2], -m_lo * e0[1]
        zero = jnp.zeros_like(d2)
        h = next_h(None, get3(e_lo, r), None)
        put_e(1, r, 0, step_e(1, r, 0, e0, get(H, r, 0), (h[1] + d2, h[2] + d3)))
        put3(lo_h, r, (zero, d2, d3))
        put3(lo_e, r, tuple(b_lo[...] * v for v in curl_h((zero, d2, d3), None)))
        e7 = e_at(0, r, 7)
        h7 = next_h(None, e7, pair(e_hi, r))
        put(H, h7, r, 7)
        put_e(1, r, 7, step_e(1, r, 7, e7, h7, (H[r, 1, 6], H[r, 2, 6])))
        c = m_hi * b_hi[...]
        put3(hi_e, r, (zero, c * h7[2], -c * h7[1]))
        do_h(1, r, 0)
        do_e(2, r, 1)
        do_h(2, r, 1)
        do_e(3, r, 2)
        do_h(1, r, 6)
        do_e(2, r, 6)
        do_h(2, r, 5)
        do_e(3, r, 5)

    runs(step2)
    lax.fori_loop(2, 6, lambda p, _: (product(p), 0)[1], 0)
    start_g(0)
    arrived(3)

    def step3_low(r):
        e0 = e_at(1, r, 0)
        de = get3(lo_e, r)
        dh = next_h(get3(lo_h, r), de, (m_lo * e0[1], m_lo * e0[2]))
        h = pair(recv_h, r)
        new = step_e(2, r, 0, e0, get(H, r, 0), (h[0] + dh[1], h[1] + dh[2]))
        put_e(2, r, 0, new)
        curl = curl_h(dh, (de[2], -de[1]))
        de = tuple(de[k] + b_lo[...] * curl[k] for k in range(3))
        dh = next_h(dh, de, (m_lo * new[1], m_lo * new[2]))
        do_h(2, r, 0)
        put_e(3, r, 0, step_e(3, r, 0, new, get(H, r, 0), (dh[1], dh[2])))
        do_e(3, r, 1)

    runs(step3_low)
    product(1)
    start_g(1)

    def step3_high(r):
        de = get3(hi_e, r)
        e = pair(recv_e, r)
        h7 = next_h(get(H, r, 7), e_at(1, r, 7), (e[0] + de[1], e[1] + de[2]))
        put(H, h7, r, 7)
        do_e(2, r, 7)
        curl = curl_h(next_h(None, de, None), (m_hi * h7[1], m_hi * h7[2]))
        de = tuple(de[k] + b_hi[...] * curl[k] for k in range(3))
        put(H, next_h(h7, e_at(2, r, 7), (de[1], de[2])), r, 7)
        do_h(2, r, 6)
        do_e(3, r, 7)
        do_e(3, r, 6)

    runs(step3_high)
    product(6)
    start_g(2)
    arrived(4)
    product(0, r_lo[...])
    start_g(3)
    product(7, r_hi[...])
    start_g(4)

    pixels = n * PIX_DEV
    ids = foot[...] - src * pixels
    total = None
    for pieces in ((0,), (1, 2), (3, 4)):
        heads, tails, chosen = [], [], []
        for piece in pieces:
            for copy in g_copies[piece]:
                copy.wait_recv()
            start, size = PIECES[piece]
            for p in range(start, start + size):
                block = G[p, share(src), :]
                for d in range(1, nsrc):
                    block = block + R[d - 1, p]
                head = block.astype(jnp.bfloat16).astype(jnp.float32)
                heads.append(head)
                tails.append(block - head)
                chosen.append(ids[p:p + 1, :])
        row = lax.broadcasted_iota(jnp.int32, (pixels, len(chosen) * ys), 0)
        select = (row == jnp.concatenate(chosen, axis=1)).astype(jnp.float32).astype(jnp.bfloat16)
        for part in (heads, tails):
            part = jnp.concatenate(part, axis=0).astype(jnp.bfloat16)
            term = jnp.dot(select, part, preferred_element_type=jnp.float32)
            total = term if total is None else total + term
    T[...] = total.reshape(n, PIX_DEV, 128)

    t_copies = [
        remote(T.at[lax.rem(me + d, n)], RT.at[d - 1], ts_sem.at[d - 1], tr_sem.at[d - 1],
               {"space": lax.rem(me + d, n)})
        for d in range(1, n)
    ]
    for copy in t_copies:
        copy.start()
    result = T[me]
    for d in range(1, n):
        t_copies[d - 1].wait_recv()
        result = result + RT[d - 1]
    out[...] = result

    for copy in t_copies:
        copy.wait_send()
    for piece in g_copies:
        for copy in piece:
            copy.wait_send()
    pl.when(has_low)(lambda: [copy.wait_send() for copy in e_copies] and None)
    pl.when(has_high)(lambda: [copy.wait_send() for copy in h_copies] and None)


def solution(mesh):
    n, nsrc = mesh.shape["space"], mesh.shape["src"]

    def per_device(fwd, adj, eps, wave, foot):
        cx, ny, nz = eps.shape
        ys = foot.shape[1]
        f32 = jnp.float32
        raw, plane = (ny, nz), (ny // 8, 8, nz)

        def vmem(*shape):
            return pltpu.VMEM(shape, f32)

        dma = pltpu.SemaphoreType.DMA
        hbm = pl.BlockSpec(memory_space=pltpu.HBM)
        return pl.pallas_call(
            functools.partial(kernel, n, nsrc),
            out_shape=jax.ShapeDtypeStruct((PIX_DEV, nz), f32),
            in_specs=[hbm, hbm, hbm, pl.BlockSpec(memory_space=pltpu.SMEM), hbm],
            out_specs=pl.BlockSpec(memory_space=pltpu.VMEM),
            scratch_shapes=[
                pltpu.VMEM(foot.shape, jnp.int32), vmem(2, 3, cx, *raw), vmem(cx, *raw),
                vmem(2, 3, cx, *plane), vmem(cx, *plane), vmem(ITERS, 2, 3, cx, *plane),
                vmem(2, 3, cx, *plane), vmem(2, 3, *plane), vmem(2, 3, *plane), vmem(2, 3, *plane),
                vmem(2, 2, *plane), vmem(2, 2, *plane), vmem(2, 2, *plane), vmem(2, 2, *plane),
                vmem(*raw), vmem(*raw), vmem(2, 3, *raw), vmem(2, 2, *raw),
                vmem(*plane), vmem(*plane), vmem(*plane), vmem(*plane), vmem(*plane), vmem(*plane),
                vmem(2, 3, *plane), vmem(2, 2, *plane),
                vmem(2, 3, *plane), vmem(2, 3, *plane), vmem(2, 3, *plane), vmem(2, 8, 128),
                vmem(cx, *raw), vmem(nsrc - 1, cx, ys, nz),
                vmem(n, PIX_DEV, nz), vmem(n - 1, PIX_DEV, nz),
                dma((4,)), dma((5,)), dma((5,)), dma((5,)), dma((5,)),
                dma((nsrc - 1, len(PIECES))), dma((nsrc - 1, len(PIECES))), dma((n - 1,)), dma((n - 1,)),
            ],
            compiler_params=pltpu.CompilerParams(
                collective_id=0, has_side_effects=True, vmem_limit_bytes=60 * 1024 * 1024),
            cost_estimate=pl.CostEstimate(flops=30_000_000, bytes_accessed=2_000_000, transcendentals=0),
        )(fwd, adj, eps, wave, foot)

    in_specs = (
        P("src", None, "space", None, None),
        P("src", None, "space", None, None),
        P("space", None, None),
        P("src"),
        P("space", "src"),
    )
    return jax.shard_map(
        per_device, mesh=mesh, in_specs=in_specs, out_specs=P(("src", "space"), None), check_vma=False)
```

```python
import functools

import jax
import jax.numpy as jnp
from jax import lax
from jax.experimental import pallas as pl
from jax.experimental.pallas import tpu as pltpu
from jax.sharding import PartitionSpec as P

ITERS = 4
PIX_DEV = 16
PIECES = ((2, 4), (1, 1), (6, 1), (0, 1), (7, 1))
MESH = pl.DeviceIdType.MESH


def ahead(f, axis):
    if axis == 1:
        return pltpu.roll(f, f.shape[2] - 1, 2)
    return jnp.concatenate([f[1:], pltpu.roll(f[:1], 7, 1)], axis=0)


def behind(f, axis):
    if axis == 1:
        return pltpu.roll(f, 1, 2)
    return jnp.concatenate([pltpu.roll(f[-1:], 1, 1), f[:-1]], axis=0)


def dealt(ref, *at):
    folds = ref.shape[-2] // 8
    return jnp.stack([ref[(*at, pl.ds(j, 8, stride=folds), slice(None))] for j in range(folds)])


def next_h(h, e, e_next):
    e1, e2, e3 = e
    x2 = -e2 if e_next is None else e_next[0] - e2
    x3 = -e3 if e_next is None else e_next[1] - e3
    curl = (
        (ahead(e3, 0) - e3) - (ahead(e2, 1) - e2),
        (ahead(e1, 1) - e1) - x3,
        x2 - (ahead(e1, 0) - e1),
    )
    if h is None:
        return tuple(-v for v in curl)
    return tuple(a - v for a, v in zip(h, curl))


def curl_h(h, h_prev):
    h1, h2, h3 = h
    x2 = h2 if h_prev is None else h2 - h_prev[0]
    x3 = h3 if h_prev is None else h3 - h_prev[1]
    return (
        (h3 - behind(h3, 0)) - (h2 - behind(h2, 1)),
        (h1 - behind(h1, 1)) - x3,
        x2 - (h1 - behind(h1, 0)),
    )


def kernel(n, nsrc, fwd, adj, eps, wave, foot_hbm, out,
           foot, JR, CR, J, C, E, H, HI, EL, EH, send_e, send_h, recv_e, recv_h, c_lo, c_hi, j_lo, j_hi,
           q_lo, q_hi, r_lo, r_hi, b_lo, b_hi, e_lo, e_hi, lo_h, lo_e, hi_e, sig, G, R, T, S, U, RT,
           load_sem, es_sem, er_sem, hs_sem, hr_sem, gs_sem, gr_sem, ss_sem, ts_sem, tr_sem):
    me = lax.axis_index("space")
    src = lax.axis_index("src")
    chips, chip, core = n // 2, me // 2, lax.rem(me, 2)
    sibling = 2 * chip + 1 - core
    low, high = lax.rem(me + n - 1, n), lax.rem(me + 1, n)
    has_low, has_high = me > 0, me < n - 1
    ys = foot.shape[1]

    loads = [
        pltpu.make_async_copy(eps, CR, load_sem.at[0]),
        pltpu.make_async_copy(fwd.at[0], JR.at[0], load_sem.at[1]),
        pltpu.make_async_copy(adj.at[0], JR.at[1], load_sem.at[2]),
        pltpu.make_async_copy(foot_hbm, foot, load_sem.at[3]),
    ]
    for copy in loads:
        copy.start()

    barrier = pltpu.get_barrier_semaphore()
    partners = [sibling, lax.rem(me + n + 2 * core - 1, n)] + [2 * lax.rem(chip + d, chips) + core for d in range(1, chips)]
    for device in partners:
        pl.semaphore_signal(barrier, inc=1, device_id={"space": device}, device_id_type=MESH)
    for d in range(1, nsrc):
        pl.semaphore_signal(barrier, inc=1, device_id={"src": lax.rem(src + d, nsrc)}, device_id_type=MESH)

    omega = 0.25 + 0.05 * wave[0].astype(jnp.float32)
    when = (lax.broadcasted_iota(jnp.int32, (8, 128), 0) + 1).astype(jnp.float32)
    sig[0] = jnp.sin(omega * when)
    sig[1] = jnp.cos(omega * when)

    def remote(a, b, s, r, where):
        return pltpu.make_async_remote_copy(
            src_ref=a, dst_ref=b, send_sem=s, recv_sem=r, device_id=where, device_id_type=MESH)

    def copies(pairs, s, r, where):
        return [remote(a, b, s.at[i], r.at[i], where) for i, (a, b) in enumerate(pairs)]

    e_copies = copies((
        (fwd.at[0, pl.ds(1, 2), 0], j_hi.at[0]), (adj.at[0, pl.ds(1, 2), 0], j_hi.at[1]), (eps.at[0], c_hi),
        (send_e, recv_e), (q_lo, r_hi)), es_sem, er_sem, {"space": low})
    h_copies = copies((
        (fwd.at[0, :, 7], j_lo.at[0]), (adj.at[0, :, 7], j_lo.at[1]), (eps.at[7], c_lo),
        (send_h, recv_h), (q_hi, r_lo)), hs_sem, hr_sem, {"space": high})

    def start_e(*those):
        pl.when(has_low)(lambda: [e_copies[i].start() for i in those] and None)

    def start_h(*those):
        pl.when(has_high)(lambda: [h_copies[i].start() for i in those] and None)

    def arrived(*those):
        pl.when(has_low)(lambda: [h_copies[i].wait_recv() for i in those] and None)
        pl.when(has_high)(lambda: [e_copies[i].wait_recv() for i in those] and None)

    @pl.when(jnp.logical_not(has_low))
    def _():
        for ref in (recv_h, c_lo, j_lo, r_lo):
            ref[...] = jnp.zeros_like(ref)

    @pl.when(jnp.logical_not(has_high))
    def _():
        for ref in (recv_e, c_hi, j_hi, r_hi):
            ref[...] = jnp.zeros_like(ref)

    m_lo = jnp.where(has_low, 1.0, 0.0).astype(jnp.float32)
    m_hi = jnp.where(has_high, 1.0, 0.0).astype(jnp.float32)

    def get(ref, *at):
        return tuple(ref[(*at[:-1], k, at[-1])] for k in range(3))

    def put(ref, vals, *at):
        for k in range(3):
            ref[(*at[:-1], k, at[-1])] = vals[k]

    def get3(ref, r):
        return tuple(ref[r, k] for k in range(3))

    def put3(ref, r, vals):
        for k in range(3):
            ref[r, k] = vals[k]

    def pair(ref, r):
        return ref[r, 0], ref[r, 1]

    def put_pair(ref, r, vals):
        ref[r, 0], ref[r, 1] = vals[1], vals[2]

    def e_at(t, r, p):
        return tuple(E[t, r, k, p] for k in range(3))

    def step_e(t, r, p, e, h, h_prev):
        c, s = C[p], sig[r, t:t + 1, :]
        curl = curl_h(h, h_prev)
        return tuple(e[k] + c * curl[k] - s * J[r, k, p] for k in range(3))

    def do_h(t, r, p):
        e, nxt = e_at(t, r, p), (E[t, r, 1, p + 1], E[t, r, 2, p + 1])
        put(H, next_h(None if t == 0 else get(H, r, p), e, nxt), r, p)

    def do_e(t, r, p):
        new = step_e(t, r, p, e_at(t - 1, r, p), get(H, r, p), (H[r, 1, p - 1], H[r, 2, p - 1]))
        for k in range(3):
            E[t, r, k, p] = new[k]

    def put_e(t, r, p, new):
        for k in range(3):
            E[t, r, k, p] = new[k]

    def runs(body):
        lax.fori_loop(0, 2, lambda r, _: (body(r), 0)[1], 0)

    def planes(first, last, body):
        def one(p, _):
            body(0, p)
            body(1, p)
            return 0

        lax.fori_loop(first, last, one, 0)

    def begin(r, p):
        c2, s = 2.0 * C[p], sig[r, 0:1, :]
        for k in range(3):
            a = c2 * dealt(JR, r, k, p)
            J[r, k, p] = a
            E[0, r, k, p] = -s * a

    pl.semaphore_wait(barrier, chips + 1 + nsrc - 1)
    start_e(0, 1, 2)
    start_h(0, 1, 2)
    for copy in loads:
        copy.wait()

    def scale(p, _):
        C[p] = 0.25 * dealt(CR, p)
        return 0

    lax.fori_loop(0, 8, scale, 0)
    planes(0, 8, begin)
    planes(0, 7, functools.partial(do_h, 0))

    def alone_low(r):
        e = step_e(1, r, 0, e_at(0, r, 0), get(H, r, 0), None)
        put3(EL, r, e)
        put_pair(send_e, r, e)

    runs(alone_low)
    start_e(3)

    def alone_high(r):
        do_e(1, r, 6)
        h7 = next_h(None, e_at(0, r, 7), None)
        e7 = step_e(1, r, 7, e_at(0, r, 7), h7, (H[r, 1, 6], H[r, 2, 6]))
        put3(EH, r, e7)
        h7 = next_h(h7, e7, None)
        put3(HI, r, h7)
        put_pair(send_h, r, h7)

    runs(alone_high)
    start_h(3)

    def alone_last(r):
        do_e(1, r, 1)
        e = get3(EL, r)
        h = next_h(get(H, r, 0), e, (E[1, r, 1, 1], E[1, r, 2, 1]))
        put3(EL, r, step_e(2, r, 0, e, h, None))
        e7, h7 = get3(EH, r), get3(HI, r)
        h6 = next_h(get(H, r, 6), e_at(1, r, 6), (e7[1], e7[2]))
        e7 = step_e(2, r, 7, e7, h7, (h6[1], h6[2]))
        put3(HI, r, next_h(h7, e7, None))

    runs(alone_last)

    planes(2, 6, functools.partial(do_e, 1))
    planes(1, 6, functools.partial(do_h, 1))
    planes(2, 6, functools.partial(do_e, 2))
    planes(2, 5, functools.partial(do_h, 2))
    planes(3, 5, functools.partial(do_e, 3))

    arrived(0, 1, 2)
    b_lo[...] = 0.25 * dealt(c_lo)
    b_hi[...] = 0.25 * dealt(c_hi)

    def edges(r):
        s = sig[r, 0:1, :]
        for k in range(3):
            e_lo[r, k] = -s * (2.0 * b_lo[...] * dealt(j_lo, r, k))
        for k in range(2):
            e_hi[r, k] = -s * (2.0 * b_hi[...] * dealt(j_hi, r, k))

    runs(edges)
    for_low, for_high = None, None
    for r in range(2):
        curl = curl_h((jnp.zeros_like(EL[r, 0]), EL[r, 2], -EL[r, 1]), None)
        terms = [e_lo[1 - r, k] * curl[k] for k in range(3)]
        term = terms[0] + terms[1] + terms[2]
        for_low = term if for_low is None else for_low + term
        term = e_hi[1 - r, 0] * HI[r, 2] - e_hi[1 - r, 1] * HI[r, 1]
        for_high = term if for_high is None else for_high + term
    q_lo[...] = b_lo[...] * for_low
    q_hi[...] = b_hi[...] * for_high
    start_e(4)
    start_h(4)

    def product(p, more=None):
        total = more
        for t in range(ITERS):
            for k in range(3):
                term = E[t, 0, k, p] * E[ITERS - 1 - t, 1, k, p]
                total = term if total is None else total + term
        folds = total.shape[0]
        for j in range(folds):
            G[p, pl.ds(j, 8, stride=folds), :] = total[j]

    def share(j):
        return pl.ds(pl.multiple_of(j * ys, 8), ys)

    g_copies = []
    for piece, (start, size) in enumerate(PIECES):
        g_copies.append([
            remote(G.at[pl.ds(start, size), share(lax.rem(src + d, nsrc))], R.at[d - 1, pl.ds(start, size)],
                   gs_sem.at[d - 1, piece], gr_sem.at[d - 1, piece], {"src": lax.rem(src + d, nsrc)})
            for d in range(1, nsrc)
        ])

    def start_g(piece):
        for copy in g_copies[piece]:
            copy.start()

    def step2(r):
        e0 = e_at(0, r, 0)
        d2, d3 = m_lo * e0[2], -m_lo * e0[1]
        zero = jnp.zeros_like(d2)
        h = next_h(None, get3(e_lo, r), None)
        put_e(1, r, 0, step_e(1, r, 0, e0, get(H, r, 0), (h[1] + d2, h[2] + d3)))
        put3(lo_h, r, (zero, d2, d3))
        put3(lo_e, r, tuple(b_lo[...] * v for v in curl_h((zero, d2, d3), None)))
        e7 = e_at(0, r, 7)
        h7 = next_h(None, e7, pair(e_hi, r))
        put(H, h7, r, 7)
        put_e(1, r, 7, step_e(1, r, 7, e7, h7, (H[r, 1, 6], H[r, 2, 6])))
        c = m_hi * b_hi[...]
        put3(hi_e, r, (zero, c * h7[2], -c * h7[1]))
        do_h(1, r, 0)
        do_e(2, r, 1)
        do_h(2, r, 1)
        do_e(3, r, 2)
        do_h(1, r, 6)
        do_e(2, r, 6)
        do_h(2, r, 5)
        do_e(3, r, 5)

    runs(step2)
    lax.fori_loop(2, 6, lambda p, _: (product(p), 0)[1], 0)
    start_g(0)
    arrived(3)

    def step3_low(r):
        e0 = e_at(1, r, 0)
        de = get3(lo_e, r)
        dh = next_h(get3(lo_h, r), de, (m_lo * e0[1], m_lo * e0[2]))
        h = pair(recv_h, r)
        new = step_e(2, r, 0, e0, get(H, r, 0), (h[0] + dh[1], h[1] + dh[2]))
        put_e(2, r, 0, new)
        curl = curl_h(dh, (de[2], -de[1]))
        de = tuple(de[k] + b_lo[...] * curl[k] for k in range(3))
        dh = next_h(dh, de, (m_lo * new[1], m_lo * new[2]))
        do_h(2, r, 0)
        put_e(3, r, 0, step_e(3, r, 0, new, get(H, r, 0), (dh[1], dh[2])))
        do_e(3, r, 1)

    runs(step3_low)
    product(1)
    start_g(1)

    def step3_high(r):
        de = get3(hi_e, r)
        e = pair(recv_e, r)
        h7 = next_h(get(H, r, 7), e_at(1, r, 7), (e[0] + de[1], e[1] + de[2]))
        put(H, h7, r, 7)
        do_e(2, r, 7)
        curl = curl_h(next_h(None, de, None), (m_hi * h7[1], m_hi * h7[2]))
        de = tuple(de[k] + b_hi[...] * curl[k] for k in range(3))
        put(H, next_h(h7, e_at(2, r, 7), (de[1], de[2])), r, 7)
        do_h(2, r, 6)
        do_e(3, r, 7)
        do_e(3, r, 6)

    runs(step3_high)
    product(6)
    start_g(2)
    arrived(4)
    product(0, r_lo[...])
    start_g(3)
    product(7, r_hi[...])
    start_g(4)

    pixels = n * PIX_DEV
    ids = foot[...] - src * pixels
    total = None
    for pieces in ((0,), (1, 2), (3, 4)):
        heads, tails, chosen = [], [], []
        for piece in pieces:
            for copy in g_copies[piece]:
                copy.wait_recv()
            start, size = PIECES[piece]
            for p in range(start, start + size):
                block = G[p, share(src), :]
                for d in range(1, nsrc):
                    block = block + R[d - 1, p]
                head = block.astype(jnp.bfloat16).astype(jnp.float32)
                heads.append(head)
                tails.append(block - head)
                chosen.append(ids[p:p + 1, :])
        row = lax.broadcasted_iota(jnp.int32, (pixels, len(chosen) * ys), 0)
        select = (row == jnp.concatenate(chosen, axis=1)).astype(jnp.float32).astype(jnp.bfloat16)
        for part in (heads, tails):
            part = jnp.concatenate(part, axis=0).astype(jnp.bfloat16)
            term = jnp.dot(select, part, preferred_element_type=jnp.float32)
            total = term if total is None else total + term
    for owner in range(n):
        T[owner % 2, owner // 2] = total[owner * PIX_DEV:(owner + 1) * PIX_DEV]
    swap = remote(T.at[1 - core], S, ss_sem.at[0], ss_sem.at[1], {"space": sibling})
    swap.start()
    swap.wait_recv()
    U[...] = T[core] + S[...]

    t_copies = [
        remote(U.at[lax.rem(chip + d, chips)], RT.at[d - 1], ts_sem.at[d - 1], tr_sem.at[d - 1],
               {"space": 2 * lax.rem(chip + d, chips) + core})
        for d in range(1, chips)
    ]
    for copy in t_copies:
        copy.start()
    result = U[chip]
    for d in range(1, chips):
        t_copies[d - 1].wait_recv()
        result = result + RT[d - 1]
    out[...] = result

    swap.wait_send()
    for copy in t_copies:
        copy.wait_send()
    for piece in g_copies:
        for copy in piece:
            copy.wait_send()
    pl.when(has_low)(lambda: [copy.wait_send() for copy in e_copies] and None)
    pl.when(has_high)(lambda: [copy.wait_send() for copy in h_copies] and None)


def solution(mesh):
    n, nsrc = mesh.shape["space"], mesh.shape["src"]

    def per_device(fwd, adj, eps, wave, foot):
        cx, ny, nz = eps.shape
        ys = foot.shape[1]
        f32 = jnp.float32
        raw, plane = (ny, nz), (ny // 8, 8, nz)

        def vmem(*shape):
            return pltpu.VMEM(shape, f32)

        dma = pltpu.SemaphoreType.DMA
        hbm = pl.BlockSpec(memory_space=pltpu.HBM)
        return pl.pallas_call(
            functools.partial(kernel, n, nsrc),
            out_shape=jax.ShapeDtypeStruct((PIX_DEV, nz), f32),
            in_specs=[hbm, hbm, hbm, pl.BlockSpec(memory_space=pltpu.SMEM), hbm],
            out_specs=pl.BlockSpec(memory_space=pltpu.VMEM),
            scratch_shapes=[
                pltpu.VMEM(foot.shape, jnp.int32), vmem(2, 3, cx, *raw), vmem(cx, *raw),
                vmem(2, 3, cx, *plane), vmem(cx, *plane), vmem(ITERS, 2, 3, cx, *plane),
                vmem(2, 3, cx, *plane), vmem(2, 3, *plane), vmem(2, 3, *plane), vmem(2, 3, *plane),
                vmem(2, 2, *plane), vmem(2, 2, *plane), vmem(2, 2, *plane), vmem(2, 2, *plane),
                vmem(*raw), vmem(*raw), vmem(2, 3, *raw), vmem(2, 2, *raw),
                vmem(*plane), vmem(*plane), vmem(*plane), vmem(*plane), vmem(*plane), vmem(*plane),
                vmem(2, 3, *plane), vmem(2, 2, *plane),
                vmem(2, 3, *plane), vmem(2, 3, *plane), vmem(2, 3, *plane), vmem(2, 8, 128),
                vmem(cx, *raw), vmem(nsrc - 1, cx, ys, nz),
                vmem(2, n // 2, PIX_DEV, nz), vmem(n // 2, PIX_DEV, nz), vmem(n // 2, PIX_DEV, nz),
                vmem(n // 2 - 1, PIX_DEV, nz),
                dma((4,)), dma((5,)), dma((5,)), dma((5,)), dma((5,)),
                dma((nsrc - 1, len(PIECES))), dma((nsrc - 1, len(PIECES))), dma((2,)), dma((n // 2 - 1,)), dma((n // 2 - 1,)),
            ],
            compiler_params=pltpu.CompilerParams(
                collective_id=0, has_side_effects=True, vmem_limit_bytes=60 * 1024 * 1024),
            cost_estimate=pl.CostEstimate(flops=30_000_000, bytes_accessed=2_000_000, transcendentals=0),
        )(fwd, adj, eps, wave, foot)

    in_specs = (
        P("src", None, "space", None, None),
        P("src", None, "space", None, None),
        P("space", None, None),
        P("src"),
        P("space", "src"),
    )
    return jax.shard_map(
        per_device, mesh=mesh, in_specs=in_specs, out_specs=P(("src", "space"), None), check_vma=False)
```

```python
import functools

import jax
import jax.numpy as jnp
from jax import lax
from jax.experimental import pallas as pl
from jax.experimental.pallas import tpu as pltpu
from jax.sharding import PartitionSpec as P

ITERS = 4
PIX_DEV = 16
PIECES = ((2, 4), (1, 1), (6, 1), (0, 1), (7, 1))
MESH = pl.DeviceIdType.MESH


def ahead(f, axis):
    if axis == 1:
        return pltpu.roll(f, f.shape[2] - 1, 2)
    return jnp.concatenate([f[1:], pltpu.roll(f[:1], 7, 1)], axis=0)


def behind(f, axis):
    if axis == 1:
        return pltpu.roll(f, 1, 2)
    return jnp.concatenate([pltpu.roll(f[-1:], 1, 1), f[:-1]], axis=0)


def dealt(ref, *at):
    folds = ref.shape[-2] // 8
    return jnp.stack([ref[(*at, pl.ds(j, 8, stride=folds), slice(None))] for j in range(folds)])


def next_h(h, e, e_next):
    e1, e2, e3 = e
    x2 = -e2 if e_next is None else e_next[0] - e2
    x3 = -e3 if e_next is None else e_next[1] - e3
    curl = (
        (ahead(e3, 0) - e3) - (ahead(e2, 1) - e2),
        (ahead(e1, 1) - e1) - x3,
        x2 - (ahead(e1, 0) - e1),
    )
    if h is None:
        return tuple(-v for v in curl)
    return tuple(a - v for a, v in zip(h, curl))


def curl_h(h, h_prev):
    h1, h2, h3 = h
    x2 = h2 if h_prev is None else h2 - h_prev[0]
    x3 = h3 if h_prev is None else h3 - h_prev[1]
    return (
        (h3 - behind(h3, 0)) - (h2 - behind(h2, 1)),
        (h1 - behind(h1, 1)) - x3,
        x2 - (h1 - behind(h1, 0)),
    )


def kernel(n, nsrc, fwd, adj, eps, wave, foot_hbm, out,
           foot, JR, CR, J, C, E, H, HI, EL, EH, send_e, send_h, recv_e, recv_h, c_lo, c_hi, j_lo, j_hi,
           q_lo, q_hi, r_lo, r_hi, b_lo, b_hi, e_lo, e_hi, lo_h, lo_e, hi_e, sig, G, R, T, S, U, RT,
           load_sem, es_sem, er_sem, hs_sem, hr_sem, gs_sem, gr_sem, ss_sem, ts_sem, tr_sem):
    me = lax.axis_index("space")
    src = lax.axis_index("src")
    chips, chip, core = n // 2, me // 2, lax.rem(me, 2)
    sibling = 2 * chip + 1 - core
    low, high = lax.rem(me + n - 1, n), lax.rem(me + 1, n)
    has_low, has_high = me > 0, me < n - 1
    ys = foot.shape[1]

    loads = [
        pltpu.make_async_copy(eps, CR, load_sem.at[0]),
        pltpu.make_async_copy(fwd.at[0], JR.at[0], load_sem.at[1]),
        pltpu.make_async_copy(adj.at[0], JR.at[1], load_sem.at[2]),
        pltpu.make_async_copy(foot_hbm, foot, load_sem.at[3]),
    ]
    for copy in loads:
        copy.start()

    barrier = pltpu.get_barrier_semaphore()
    partners = [sibling, lax.rem(me + n + 2 * core - 1, n)] + [2 * lax.rem(chip + d, chips) + core for d in range(1, chips)]
    for device in partners:
        pl.semaphore_signal(barrier, inc=1, device_id={"space": device}, device_id_type=MESH)
    for d in range(1, nsrc):
        pl.semaphore_signal(barrier, inc=1, device_id={"src": lax.rem(src + d, nsrc)}, device_id_type=MESH)

    omega = 0.25 + 0.05 * wave[0].astype(jnp.float32)
    when = (lax.broadcasted_iota(jnp.int32, (8, 128), 0) + 1).astype(jnp.float32)
    sig[0] = jnp.sin(omega * when)
    sig[1] = jnp.cos(omega * when)

    def remote(a, b, s, r, where):
        return pltpu.make_async_remote_copy(
            src_ref=a, dst_ref=b, send_sem=s, recv_sem=r, device_id=where, device_id_type=MESH)

    def copies(pairs, s, r, where):
        return [remote(a, b, s.at[i], r.at[i], where) for i, (a, b) in enumerate(pairs)]

    e_copies = copies((
        (fwd.at[0, pl.ds(1, 2), 0], j_hi.at[0]), (adj.at[0, pl.ds(1, 2), 0], j_hi.at[1]), (eps.at[0], c_hi),
        (send_e, recv_e), (q_lo, r_hi)), es_sem, er_sem, {"space": low})
    h_copies = copies((
        (fwd.at[0, :, 7], j_lo.at[0]), (adj.at[0, :, 7], j_lo.at[1]), (eps.at[7], c_lo),
        (send_h, recv_h), (q_hi, r_lo)), hs_sem, hr_sem, {"space": high})

    def start_e(*those):
        pl.when(has_low)(lambda: [e_copies[i].start() for i in those] and None)

    def start_h(*those):
        pl.when(has_high)(lambda: [h_copies[i].start() for i in those] and None)

    def arrived(*those):
        pl.when(has_low)(lambda: [h_copies[i].wait_recv() for i in those] and None)
        pl.when(has_high)(lambda: [e_copies[i].wait_recv() for i in those] and None)

    @pl.when(jnp.logical_not(has_low))
    def _():
        for ref in (recv_h, c_lo, j_lo, r_lo):
            ref[...] = jnp.zeros_like(ref)

    @pl.when(jnp.logical_not(has_high))
    def _():
        for ref in (recv_e, c_hi, j_hi, r_hi):
            ref[...] = jnp.zeros_like(ref)

    m_lo = jnp.where(has_low, 1.0, 0.0).astype(jnp.float32)
    m_hi = jnp.where(has_high, 1.0, 0.0).astype(jnp.float32)

    def get(ref, *at):
        return tuple(ref[(*at[:-1], k, at[-1])] for k in range(3))

    def put(ref, vals, *at):
        for k in range(3):
            ref[(*at[:-1], k, at[-1])] = vals[k]

    def get3(ref, r):
        return tuple(ref[r, k] for k in range(3))

    def put3(ref, r, vals):
        for k in range(3):
            ref[r, k] = vals[k]

    def pair(ref, r):
        return ref[r, 0], ref[r, 1]

    def put_pair(ref, r, vals):
        ref[r, 0], ref[r, 1] = vals[1], vals[2]

    def e_at(t, r, p):
        return tuple(E[t, r, k, p] for k in range(3))

    def step_e(t, r, p, e, h, h_prev):
        c, s = C[p], sig[r, t:t + 1, :]
        curl = curl_h(h, h_prev)
        return tuple(e[k] + c * curl[k] - s * J[r, k, p] for k in range(3))

    def h_at(r, p):
        return tuple(H[r, k, p] for k in range(3))

    def new_h(t, r, p):
        return next_h(None if t == 0 else h_at(r, p), e_at(t, r, p), (E[t, r, 1, p + 1], E[t, r, 2, p + 1]))

    def put_e(t, r, p, new):
        for k in range(3):
            E[t, r, k, p] = new[k]

    def runs(body):
        lax.fori_loop(0, 2, lambda r, _: (body(r), 0)[1], 0)

    def planes(first, last, body):
        lax.fori_loop(first, last, lambda p, _: (body(p), 0)[1], 0)

    def sweep(t, first, last):
        hs = [new_h(t, r, first) for r in range(2)]
        for r in range(2):
            put(H, hs[r], r, first)

        def body(p):
            hs = [new_h(t, r, p) for r in range(2)]
            es = [step_e(t + 1, r, p, e_at(t, r, p), hs[r], (H[r, 1, p - 1], H[r, 2, p - 1])) for r in range(2)]
            for r in range(2):
                put(H, hs[r], r, p)
                put_e(t + 1, r, p, es[r])

        planes(first + 1, last, body)

    def begin(p):
        c = 0.25 * dealt(CR, p)
        for r in range(2):
            s = sig[r, 0:1, :]
            for k in range(3):
                a = 2.0 * c * dealt(JR, r, k, p)
                J[r, k, p] = a
                E[0, r, k, p] = -s * a
        C[p] = c

    pl.semaphore_wait(barrier, chips + 1 + nsrc - 1)
    start_e(0, 1, 2)
    start_h(0, 1, 2)
    for copy in loads:
        copy.wait()

    planes(0, 8, begin)
    sweep(0, 0, 7)

    def alone(r):
        h0, h6, e1, e2, e3 = h_at(r, 0), h_at(r, 6), e_at(0, r, 0), e_at(1, r, 1), e_at(0, r, 7)
        e6 = e_at(1, r, 6)
        h7 = next_h(None, e3, None)
        e7 = step_e(1, r, 7, e3, h7, h6[1:])
        h7 = next_h(h7, e7, None)
        e0 = step_e(1, r, 0, e1, h0, None)
        put_pair(send_e, r, e0)
        put_pair(send_h, r, h7)
        put3(EL, r, step_e(2, r, 0, e0, next_h(h0, e0, e2[1:]), None))
        h6 = next_h(h6, e6, e7[1:])
        put3(HI, r, next_h(h7, step_e(2, r, 7, e7, h7, h6[1:]), None))

    runs(alone)
    start_e(3)
    start_h(3)
    sweep(1, 1, 6)
    sweep(2, 2, 5)

    arrived(0, 1, 2)
    b_lo[...] = 0.25 * dealt(c_lo)
    b_hi[...] = 0.25 * dealt(c_hi)

    def edges(r):
        s = sig[r, 0:1, :]
        for k in range(3):
            e_lo[r, k] = -s * (2.0 * b_lo[...] * dealt(j_lo, r, k))
        for k in range(2):
            e_hi[r, k] = -s * (2.0 * b_hi[...] * dealt(j_hi, r, k))

    runs(edges)
    for_low, for_high = None, None
    for r in range(2):
        curl = curl_h((jnp.zeros_like(EL[r, 0]), EL[r, 2], -EL[r, 1]), None)
        terms = [e_lo[1 - r, k] * curl[k] for k in range(3)]
        term = terms[0] + terms[1] + terms[2]
        for_low = term if for_low is None else for_low + term
        term = e_hi[1 - r, 0] * HI[r, 2] - e_hi[1 - r, 1] * HI[r, 1]
        for_high = term if for_high is None else for_high + term
    q_lo[...] = b_lo[...] * for_low
    q_hi[...] = b_hi[...] * for_high
    start_e(4)
    start_h(4)

    def product(p, more=None):
        total = more
        for t in range(ITERS):
            for k in range(3):
                term = E[t, 0, k, p] * E[ITERS - 1 - t, 1, k, p]
                total = term if total is None else total + term
        folds = total.shape[0]
        for j in range(folds):
            G[p, pl.ds(j, 8, stride=folds), :] = total[j]

    def share(j):
        return pl.ds(pl.multiple_of(j * ys, 8), ys)

    g_copies = []
    for piece, (start, size) in enumerate(PIECES):
        g_copies.append([
            remote(G.at[pl.ds(start, size), share(lax.rem(src + d, nsrc))], R.at[d - 1, pl.ds(start, size)],
                   gs_sem.at[d - 1, piece], gr_sem.at[d - 1, piece], {"src": lax.rem(src + d, nsrc)})
            for d in range(1, nsrc)
        ])

    def start_g(piece):
        for copy in g_copies[piece]:
            copy.start()

    def step2(r):
        e0, e7, h0, h1, h5, h6 = e_at(0, r, 0), e_at(0, r, 7), h_at(r, 0), h_at(r, 1), h_at(r, 5), h_at(r, 6)
        e1, e6, f2, f5 = e_at(1, r, 1), e_at(1, r, 6), e_at(2, r, 2), e_at(2, r, 5)
        d2, d3 = m_lo * e0[2], -m_lo * e0[1]
        zero = jnp.zeros_like(d2)
        h = next_h(None, get3(e_lo, r), None)
        e0 = step_e(1, r, 0, e0, h0, (h[1] + d2, h[2] + d3))
        de = tuple(b_lo[...] * v for v in curl_h((zero, d2, d3), None))
        h0 = next_h(h0, e0, e1[1:])
        f1 = step_e(2, r, 1, e1, h1, h0[1:])
        h1 = next_h(h1, f1, f2[1:])
        g2 = step_e(3, r, 2, f2, h_at(r, 2), h1[1:])
        h7 = next_h(None, e7, pair(e_hi, r))
        e7 = step_e(1, r, 7, e7, h7, h6[1:])
        c = m_hi * b_hi[...]
        h6 = next_h(h6, e6, e7[1:])
        f6 = step_e(2, r, 6, e6, h6, h5[1:])
        h5 = next_h(h5, f5, f6[1:])
        g5 = step_e(3, r, 5, f5, h5, (H[r, 1, 4], H[r, 2, 4]))
        put3(lo_h, r, (zero, d2, d3))
        put3(lo_e, r, de)
        put3(hi_e, r, (zero, c * h7[2], -c * h7[1]))
        for p, h in ((0, h0), (1, h1), (5, h5), (6, h6), (7, h7)):
            put(H, h, r, p)
        for t, p, e in ((1, 0, e0), (2, 1, f1), (3, 2, g2), (1, 7, e7), (2, 6, f6), (3, 5, g5)):
            put_e(t, r, p, e)

    runs(step2)
    lax.fori_loop(2, 6, lambda p, _: (product(p), 0)[1], 0)
    start_g(0)
    arrived(3)

    def step3(r):
        e0, e7, f1, f6 = e_at(1, r, 0), e_at(1, r, 7), e_at(2, r, 1), e_at(2, r, 6)
        h0, h6, h7 = h_at(r, 0), h_at(r, 6), h_at(r, 7)
        de, dh = get3(lo_e, r), get3(lo_h, r)
        dh = next_h(dh, de, (m_lo * e0[1], m_lo * e0[2]))
        h = pair(recv_h, r)
        f0 = step_e(2, r, 0, e0, h0, (h[0] + dh[1], h[1] + dh[2]))
        curl = curl_h(dh, (de[2], -de[1]))
        de = tuple(de[k] + b_lo[...] * curl[k] for k in range(3))
        dh = next_h(dh, de, (m_lo * f0[1], m_lo * f0[2]))
        h0 = next_h(h0, f0, f1[1:])
        g0 = step_e(3, r, 0, f0, h0, dh[1:])
        g1 = step_e(3, r, 1, f1, h_at(r, 1), h0[1:])
        de, e = get3(hi_e, r), pair(recv_e, r)
        h7 = next_h(h7, e7, (e[0] + de[1], e[1] + de[2]))
        f7 = step_e(2, r, 7, e7, h7, h6[1:])
        curl = curl_h(next_h(None, de, None), (m_hi * h7[1], m_hi * h7[2]))
        de = tuple(de[k] + b_hi[...] * curl[k] for k in range(3))
        h7 = next_h(h7, f7, de[1:])
        h6 = next_h(h6, f6, f7[1:])
        g7 = step_e(3, r, 7, f7, h7, h6[1:])
        g6 = step_e(3, r, 6, f6, h6, (H[r, 1, 5], H[r, 2, 5]))
        for t, p, e in ((2, 0, f0), (3, 0, g0), (3, 1, g1), (2, 7, f7), (3, 7, g7), (3, 6, g6)):
            put_e(t, r, p, e)

    runs(step3)
    product(1)
    start_g(1)
    product(6)
    start_g(2)
    arrived(4)
    product(0, r_lo[...])
    start_g(3)
    product(7, r_hi[...])
    start_g(4)

    pixels = n * PIX_DEV
    ids = foot[...] - src * pixels
    total = None
    for pieces in ((0,), (1, 2), (3, 4)):
        heads, tails, chosen = [], [], []
        for piece in pieces:
            for copy in g_copies[piece]:
                copy.wait_recv()
            start, size = PIECES[piece]
            for p in range(start, start + size):
                block = G[p, share(src), :]
                for d in range(1, nsrc):
                    block = block + R[d - 1, p]
                head = block.astype(jnp.bfloat16).astype(jnp.float32)
                heads.append(head)
                tails.append(block - head)
                chosen.append(ids[p:p + 1, :])
        row = lax.broadcasted_iota(jnp.int32, (pixels, len(chosen) * ys), 0)
        select = (row == jnp.concatenate(chosen, axis=1)).astype(jnp.float32).astype(jnp.bfloat16)
        for part in (heads, tails):
            part = jnp.concatenate(part, axis=0).astype(jnp.bfloat16)
            term = jnp.dot(select, part, preferred_element_type=jnp.float32)
            total = term if total is None else total + term
    for owner in range(n):
        T[owner % 2, owner // 2] = total[owner * PIX_DEV:(owner + 1) * PIX_DEV]
    swap = remote(T.at[1 - core], S, ss_sem.at[0], ss_sem.at[1], {"space": sibling})
    swap.start()
    swap.wait_recv()
    U[...] = T[core] + S[...]

    t_copies = [
        remote(U.at[lax.rem(chip + d, chips)], RT.at[d - 1], ts_sem.at[d - 1], tr_sem.at[d - 1],
               {"space": 2 * lax.rem(chip + d, chips) + core})
        for d in range(1, chips)
    ]
    for copy in t_copies:
        copy.start()
    result = U[chip]
    for d in range(1, chips):
        t_copies[d - 1].wait_recv()
        result = result + RT[d - 1]
    out[...] = result

    swap.wait_send()
    for copy in t_copies:
        copy.wait_send()
    for piece in g_copies:
        for copy in piece:
            copy.wait_send()
    pl.when(has_low)(lambda: [copy.wait_send() for copy in e_copies] and None)
    pl.when(has_high)(lambda: [copy.wait_send() for copy in h_copies] and None)


def solution(mesh):
    n, nsrc = mesh.shape["space"], mesh.shape["src"]

    def per_device(fwd, adj, eps, wave, foot):
        cx, ny, nz = eps.shape
        ys = foot.shape[1]
        f32 = jnp.float32
        raw, plane = (ny, nz), (ny // 8, 8, nz)

        def vmem(*shape):
            return pltpu.VMEM(shape, f32)

        dma = pltpu.SemaphoreType.DMA
        hbm = pl.BlockSpec(memory_space=pltpu.HBM)
        return pl.pallas_call(
            functools.partial(kernel, n, nsrc),
            out_shape=jax.ShapeDtypeStruct((PIX_DEV, nz), f32),
            in_specs=[hbm, hbm, hbm, pl.BlockSpec(memory_space=pltpu.SMEM), hbm],
            out_specs=pl.BlockSpec(memory_space=pltpu.VMEM),
            scratch_shapes=[
                pltpu.VMEM(foot.shape, jnp.int32), vmem(2, 3, cx, *raw), vmem(cx, *raw),
                vmem(2, 3, cx, *plane), vmem(cx, *plane), vmem(ITERS, 2, 3, cx, *plane),
                vmem(2, 3, cx, *plane), vmem(2, 3, *plane), vmem(2, 3, *plane), vmem(2, 3, *plane),
                vmem(2, 2, *plane), vmem(2, 2, *plane), vmem(2, 2, *plane), vmem(2, 2, *plane),
                vmem(*raw), vmem(*raw), vmem(2, 3, *raw), vmem(2, 2, *raw),
                vmem(*plane), vmem(*plane), vmem(*plane), vmem(*plane), vmem(*plane), vmem(*plane),
                vmem(2, 3, *plane), vmem(2, 2, *plane),
                vmem(2, 3, *plane), vmem(2, 3, *plane), vmem(2, 3, *plane), vmem(2, 8, 128),
                vmem(cx, *raw), vmem(nsrc - 1, cx, ys, nz),
                vmem(2, n // 2, PIX_DEV, nz), vmem(n // 2, PIX_DEV, nz), vmem(n // 2, PIX_DEV, nz),
                vmem(n // 2 - 1, PIX_DEV, nz),
                dma((4,)), dma((5,)), dma((5,)), dma((5,)), dma((5,)),
                dma((nsrc - 1, len(PIECES))), dma((nsrc - 1, len(PIECES))), dma((2,)), dma((n // 2 - 1,)), dma((n // 2 - 1,)),
            ],
            compiler_params=pltpu.CompilerParams(
                collective_id=0, has_side_effects=True, vmem_limit_bytes=60 * 1024 * 1024),
            cost_estimate=pl.CostEstimate(flops=30_000_000, bytes_accessed=2_000_000, transcendentals=0),
        )(fwd, adj, eps, wave, foot)

    in_specs = (
        P("src", None, "space", None, None),
        P("src", None, "space", None, None),
        P("space", None, None),
        P("src"),
        P("space", "src"),
    )
    return jax.shard_map(
        per_device, mesh=mesh, in_specs=in_specs, out_specs=P(("src", "space"), None), check_vma=False)
```

```python
import functools

import jax
import jax.numpy as jnp
from jax import lax
from jax.experimental import pallas as pl
from jax.experimental.pallas import tpu as pltpu
from jax.sharding import PartitionSpec as P

ITERS = 4
PIX_DEV = 16
PIECES = ((3, 2), (1, 2), (5, 2), (0, 1), (7, 1))
MESH = pl.DeviceIdType.MESH


def ahead(f, axis):
    if axis == 1:
        return pltpu.roll(f, f.shape[2] - 1, 2)
    return jnp.concatenate([f[1:], pltpu.roll(f[:1], 7, 1)], axis=0)


def behind(f, axis):
    if axis == 1:
        return pltpu.roll(f, 1, 2)
    return jnp.concatenate([pltpu.roll(f[-1:], 1, 1), f[:-1]], axis=0)


def dealt(ref, *at):
    folds = ref.shape[-2] // 8
    return jnp.stack([ref[(*at, pl.ds(j, 8, stride=folds), slice(None))] for j in range(folds)])


def next_h(h, e, e_next):
    e1, e2, e3 = e
    x2 = -e2 if e_next is None else e_next[0] - e2
    x3 = -e3 if e_next is None else e_next[1] - e3
    curl = (
        (ahead(e3, 0) - e3) - (ahead(e2, 1) - e2),
        (ahead(e1, 1) - e1) - x3,
        x2 - (ahead(e1, 0) - e1),
    )
    if h is None:
        return tuple(-v for v in curl)
    return tuple(a - v for a, v in zip(h, curl))


def curl_h(h, h_prev):
    h1, h2, h3 = h
    x2 = h2 if h_prev is None else h2 - h_prev[0]
    x3 = h3 if h_prev is None else h3 - h_prev[1]
    return (
        (h3 - behind(h3, 0)) - (h2 - behind(h2, 1)),
        (h1 - behind(h1, 1)) - x3,
        x2 - (h1 - behind(h1, 0)),
    )


def kernel(n, nsrc, fwd, adj, eps, wave, foot_hbm, out,
           foot, JR, CR, J, C, E, H, DE, DH, XE, XH, c_lo, c_hi, j_lo, j_hi,
           q_lo, q_hi, RQ, e_lo, sig, G, R, T, S, U, RT,
           load_sem, es_sem, er_sem, hs_sem, hr_sem, gs_sem, gr_sem, ss_sem, ts_sem, tr_sem):
    me = lax.axis_index("space")
    src = lax.axis_index("src")
    chips, chip, core = n // 2, me // 2, lax.rem(me, 2)
    sibling = 2 * chip + 1 - core
    low, high = lax.rem(me + n - 1, n), lax.rem(me + 1, n)
    has_low, has_high = me > 0, me < n - 1
    ys = foot.shape[1]

    loads = [
        pltpu.make_async_copy(eps, CR, load_sem.at[0]),
        pltpu.make_async_copy(fwd.at[0], JR.at[0], load_sem.at[1]),
        pltpu.make_async_copy(adj.at[0], JR.at[1], load_sem.at[2]),
        pltpu.make_async_copy(foot_hbm, foot, load_sem.at[3]),
    ]
    for copy in loads:
        copy.start()

    barrier = pltpu.get_barrier_semaphore()
    partners = [sibling, lax.rem(me + n + 2 * core - 1, n)] + [2 * lax.rem(chip + d, chips) + core for d in range(1, chips)]
    for device in partners:
        pl.semaphore_signal(barrier, inc=1, device_id={"space": device}, device_id_type=MESH)
    for d in range(1, nsrc):
        pl.semaphore_signal(barrier, inc=1, device_id={"src": lax.rem(src + d, nsrc)}, device_id_type=MESH)

    omega = 0.25 + 0.05 * wave[0].astype(jnp.float32)
    when = (lax.broadcasted_iota(jnp.int32, (8, 128), 0) + 1).astype(jnp.float32)
    sig[0] = jnp.sin(omega * when)
    sig[1] = jnp.cos(omega * when)

    def remote(a, b, s, r, where):
        return pltpu.make_async_remote_copy(
            src_ref=a, dst_ref=b, send_sem=s, recv_sem=r, device_id=where, device_id_type=MESH)

    def copies(pairs, s, r, where):
        return [remote(a, b, s.at[i], r.at[i], where) for i, (a, b) in enumerate(pairs)]

    e_copies = copies((
        (fwd.at[0, pl.ds(1, 2), 0], j_hi.at[0]), (adj.at[0, pl.ds(1, 2), 0], j_hi.at[1]), (eps.at[0], c_hi),
        (XE.at[1, 0], XE.at[1, 1]), (q_lo, RQ.at[1])), es_sem, er_sem, {"space": low})
    h_copies = copies((
        (fwd.at[0, :, 7], j_lo.at[0]), (adj.at[0, :, 7], j_lo.at[1]), (eps.at[7], c_lo),
        (XH.at[1, 1], XH.at[1, 0]), (q_hi, RQ.at[0])), hs_sem, hr_sem, {"space": high})

    def start_e(*those):
        pl.when(has_low)(lambda: [e_copies[i].start() for i in those] and None)

    def start_h(*those):
        pl.when(has_high)(lambda: [h_copies[i].start() for i in those] and None)

    def arrived(*those):
        pl.when(has_low)(lambda: [h_copies[i].wait_recv() for i in those] and None)
        pl.when(has_high)(lambda: [e_copies[i].wait_recv() for i in those] and None)

    @pl.when(jnp.logical_not(has_low))
    def _():
        for ref in (XH.at[1, 0], c_lo, j_lo, RQ.at[0]):
            ref[...] = jnp.zeros(ref.shape, jnp.float32)

    @pl.when(jnp.logical_not(has_high))
    def _():
        for ref in (XE.at[1, 1], c_hi, j_hi, RQ.at[1]):
            ref[...] = jnp.zeros(ref.shape, jnp.float32)

    m_lo = jnp.where(has_low, 1.0, 0.0).astype(jnp.float32)
    m_hi = jnp.where(has_high, 1.0, 0.0).astype(jnp.float32)

    def three(ref, *at):
        return tuple(ref[(*at[:-1], k, at[-1])] for k in range(3))

    def put(ref, vals, *at):
        for k in range(3):
            ref[(*at[:-1], k, at[-1])] = vals[k]

    def loop(first, last, body):
        lax.fori_loop(first, last, lambda i, _: (body(i), 0)[1], 0)

    zero = jnp.zeros(C.shape[1:], jnp.float32)

    def begin(p):
        c = 0.25 * dealt(CR, p)
        for r in range(2):
            s = sig[r, 0:1, :]
            for k in range(3):
                a = 2.0 * c * dealt(JR, r, k, p)
                J[r, k, p] = a
                E[0, r, k, p + 1] = -s * a
                H[r, k, p + 1] = zero
        C[p + 3] = c

    def clear(i):
        for r in range(2):
            for k in range(3):
                DE[i // 7, r, k, i % 7] = zero
                DH[i // 7, r, k, i % 7] = zero

    def clear_outside(t):
        for r in range(2):
            for k in range(3):
                E[t, r, k, 9] = zero
                E[t, r, k, 0] = zero
                H[r, k, 0] = zero
            for k in range(2):
                XE[2, 1, r, k] = zero
                XH[2, 0, r, k] = zero

    pl.semaphore_wait(barrier, chips + 1 + nsrc - 1)
    start_e(0, 1, 2)
    start_h(0, 1, 2)
    for copy in loads:
        copy.wait()

    loop(0, 4, clear_outside)
    loop(0, 8, begin)
    for r in range(2):
        for k in range(2):
            XE[0, 0, r, k] = E[0, r, 1 + k, 1]

    def alone(t):
        def body(p):
            es = [three(E, t - 1, r, p + 1) for r in range(2)]
            hs = [next_h(three(H, r, p + 1), es[r], tuple(E[t - 1, r, k, p + 2] for k in (1, 2))) for r in range(2)]
            new = []
            for r in range(2):
                curl, s = curl_h(hs[r], (H[r, 1, p], H[r, 2, p])), sig[r, pl.ds(t, 1), :]
                new.append(tuple(es[r][k] + C[p + 3] * curl[k] - s * J[r, k, p] for k in range(3)))
            for r in range(2):
                put(H, hs[r], r, p + 1)
                put(E, new[r], t, r, p + 1)

        loop(0, 8, body)
        for r in range(2):
            for k in range(2):
                XH[t - 1, 1, r, k] = H[r, 1 + k, 8]

        @pl.when(t < 3)
        def _():
            for r in range(2):
                for k in range(2):
                    XE[t, 0, r, k] = E[t, r, 1 + k, 1]

        @pl.when(t == 2)
        def _():
            start_e(3)
            start_h(3)

    loop(1, ITERS, alone)
    loop(0, 14, clear)

    arrived(0, 1, 2)
    C[2] = 0.25 * dealt(c_lo)
    C[11] = 0.25 * dealt(c_hi)

    def edges(r):
        s = sig[r, 0:1, :]
        low_c, high_c = -2.0 * s * C[2], -2.0 * s * C[11]
        e = tuple(low_c * dealt(j_lo, r, k) for k in range(3))
        h = next_h(None, e, None)
        for k in range(3):
            e_lo[r, k] = e[k]
        for k in range(2):
            XE[0, 1, r, k] = high_c * dealt(j_hi, r, k)
            XH[0, 0, r, k] = h[1 + k]

    loop(0, 2, edges)
    for_low, for_high = None, None
    for r in range(2):
        curl = curl_h((zero, XE[2, 0, r, 1], -XE[2, 0, r, 0]), None)
        terms = [e_lo[1 - r, k] * curl[k] for k in range(3)]
        term = terms[0] + terms[1] + terms[2]
        for_low = term if for_low is None else for_low + term
        term = XE[0, 1, 1 - r, 0] * XH[2, 1, r, 1] - XE[0, 1, 1 - r, 1] * XH[2, 1, r, 0]
        for_high = term if for_high is None else for_high + term
    q_lo[...] = C[2] * for_low
    q_hi[...] = C[11] * for_high
    start_e(4)
    start_h(4)

    def product(p, more=None):
        total = more
        for t in range(ITERS):
            for k in range(3):
                term = E[t, 0, k, p + 1] * E[ITERS - 1 - t, 1, k, p + 1]
                total = term if total is None else total + term
        folds = total.shape[0]
        for j in range(folds):
            G[p, pl.ds(j, 8, stride=folds), :] = total[j]

    def share(j):
        return pl.ds(pl.multiple_of(j * ys, 8), ys)

    g_copies = []
    for piece, (start, size) in enumerate(PIECES):
        g_copies.append([
            remote(G.at[pl.ds(start, size), share(lax.rem(src + d, nsrc))], R.at[d - 1, pl.ds(start, size)],
                   gs_sem.at[d - 1, piece], gr_sem.at[d - 1, piece], {"src": lax.rem(src + d, nsrc)})
            for d in range(1, nsrc)
        ])

    def start_g(piece):
        for copy in g_copies[piece]:
            copy.start()

    loop(3, 5, product)
    start_g(0)

    def correct(t, side):
        is_low = side == 0
        own_e = jnp.where(is_low, m_lo, 1.0)
        own_h = jnp.where(is_low, 1.0, m_hi)

        def magnetic(i):
            m = jnp.where(i == 2, own_e, 0.0)
            hs = []
            for r in range(2):
                nxt = tuple(DE[side, r, 1 + k, i + 1] + m * XE[t - 1, side, r, k] for k in range(2))
                hs.append(next_h(three(DH, side, r, i + 1), three(DE, side, r, i), nxt))
            for r in range(2):
                put(DH, hs[r], side, r, i + 1)

        def electric(i):
            m = jnp.where(i == 3, own_h, 0.0)
            c = C[8 * side + i]
            new = []
            for r in range(2):
                prev = tuple(DH[side, r, 1 + k, i] + m * XH[t - 1, side, r, k] for k in range(2))
                curl = curl_h(three(DH, side, r, i + 1), prev)
                d = three(DE, side, r, i)
                d = tuple(d[k] + c * curl[k] for k in range(3))
                e = three(E, t, r, 8 * side + i - 2)
                new.append((d, tuple(e[k] + d[k] for k in range(3))))
            for r in range(2):
                put(DE, new[r][0], side, r, i)
                put(E, new[r][1], t, r, 8 * side + i - 2)

        last = t == 3
        loop(jnp.where(is_low, jnp.where(t == 2, 1, 2), 3 - t),
             jnp.where(is_low, t + 2, jnp.where(t == 2, 4, 3)), magnetic)
        loop(jnp.where(is_low, jnp.where(last, 3, 2), 3 - t),
             jnp.where(is_low, t + 3, jnp.where(last, 3, 4)), electric)

    def correct_step(t):
        pl.when(t == 2)(lambda: arrived(3))
        loop(0, 2, functools.partial(correct, t))

    loop(1, ITERS, correct_step)
    loop(0, 4, lambda i: product(jnp.where(i < 2, i + 1, i + 3)))
    start_g(1)
    start_g(2)
    arrived(4)
    loop(0, 2, lambda i: product(7 * i, RQ[i]))
    start_g(3)
    start_g(4)

    pixels = n * PIX_DEV
    ids = foot[...] - src * pixels
    total = None
    for pieces in ((0, 1, 2), (3, 4)):
        heads, tails, chosen = [], [], []
        for piece in pieces:
            for copy in g_copies[piece]:
                copy.wait_recv()
            start, size = PIECES[piece]
            for p in range(start, start + size):
                block = G[p, share(src), :]
                for d in range(1, nsrc):
                    block = block + R[d - 1, p]
                head = block.astype(jnp.bfloat16).astype(jnp.float32)
                heads.append(head)
                tails.append(block - head)
                chosen.append(ids[p:p + 1, :])
        row = lax.broadcasted_iota(jnp.int32, (pixels, len(chosen) * ys), 0)
        select = (row == jnp.concatenate(chosen, axis=1)).astype(jnp.float32).astype(jnp.bfloat16)
        for part in (heads, tails):
            part = jnp.concatenate(part, axis=0).astype(jnp.bfloat16)
            term = jnp.dot(select, part, preferred_element_type=jnp.float32)
            total = term if total is None else total + term
    for owner in range(n):
        T[owner % 2, owner // 2] = total[owner * PIX_DEV:(owner + 1) * PIX_DEV]
    swap = remote(T.at[1 - core], S, ss_sem.at[0], ss_sem.at[1], {"space": sibling})
    swap.start()
    swap.wait_recv()
    U[...] = T[core] + S[...]

    t_copies = [
        remote(U.at[lax.rem(chip + d, chips)], RT.at[d - 1], ts_sem.at[d - 1], tr_sem.at[d - 1],
               {"space": 2 * lax.rem(chip + d, chips) + core})
        for d in range(1, chips)
    ]
    for copy in t_copies:
        copy.start()
    result = U[chip]
    for d in range(1, chips):
        t_copies[d - 1].wait_recv()
        result = result + RT[d - 1]
    out[...] = result

    swap.wait_send()
    for copy in t_copies:
        copy.wait_send()
    for piece in g_copies:
        for copy in piece:
            copy.wait_send()
    pl.when(has_low)(lambda: [copy.wait_send() for copy in e_copies] and None)
    pl.when(has_high)(lambda: [copy.wait_send() for copy in h_copies] and None)


def solution(mesh):
    n, nsrc = mesh.shape["space"], mesh.shape["src"]

    def per_device(fwd, adj, eps, wave, foot):
        cx, ny, nz = eps.shape
        ys = foot.shape[1]
        f32 = jnp.float32
        raw, plane = (ny, nz), (ny // 8, 8, nz)

        def vmem(*shape):
            return pltpu.VMEM(shape, f32)

        dma = pltpu.SemaphoreType.DMA
        hbm = pl.BlockSpec(memory_space=pltpu.HBM)
        return pl.pallas_call(
            functools.partial(kernel, n, nsrc),
            out_shape=jax.ShapeDtypeStruct((PIX_DEV, nz), f32),
            in_specs=[hbm, hbm, hbm, pl.BlockSpec(memory_space=pltpu.SMEM), hbm],
            out_specs=pl.BlockSpec(memory_space=pltpu.VMEM),
            scratch_shapes=[
                pltpu.VMEM(foot.shape, jnp.int32), vmem(2, 3, cx, *raw), vmem(cx, *raw),
                vmem(2, 3, cx, *plane), vmem(cx + 4, *plane), vmem(ITERS, 2, 3, cx + 2, *plane),
                vmem(2, 3, cx + 1, *plane), vmem(2, 2, 3, 7, *plane), vmem(2, 2, 3, 7, *plane),
                vmem(3, 2, 2, 2, *plane), vmem(3, 2, 2, 2, *plane),
                vmem(*raw), vmem(*raw), vmem(2, 3, *raw), vmem(2, 2, *raw),
                vmem(*plane), vmem(*plane), vmem(2, *plane), vmem(2, 3, *plane), vmem(2, 8, 128),
                vmem(cx, *raw), vmem(nsrc - 1, cx, ys, nz),
                vmem(2, n // 2, PIX_DEV, nz), vmem(n // 2, PIX_DEV, nz), vmem(n // 2, PIX_DEV, nz),
                vmem(n // 2 - 1, PIX_DEV, nz),
                dma((4,)), dma((5,)), dma((5,)), dma((5,)), dma((5,)),
                dma((nsrc - 1, len(PIECES))), dma((nsrc - 1, len(PIECES))), dma((2,)), dma((n // 2 - 1,)), dma((n // 2 - 1,)),
            ],
            compiler_params=pltpu.CompilerParams(
                collective_id=0, has_side_effects=True, vmem_limit_bytes=60 * 1024 * 1024),
            cost_estimate=pl.CostEstimate(flops=30_000_000, bytes_accessed=2_000_000, transcendentals=0),
        )(fwd, adj, eps, wave, foot)

    in_specs = (
        P("src", None, "space", None, None),
        P("src", None, "space", None, None),
        P("space", None, None),
        P("src"),
        P("space", "src"),
    )
    return jax.shard_map(
        per_device, mesh=mesh, in_specs=in_specs, out_specs=P(("src", "space"), None), check_vma=False)
```

```python
import functools

import jax
import jax.numpy as jnp
from jax import lax
from jax.experimental import pallas as pl
from jax.experimental.pallas import tpu as pltpu
from jax.sharding import PartitionSpec as P

ITERS = 4
PIX_DEV = 16
PIECES = ((2, 4), (1, 1), (6, 1), (0, 1), (7, 1))
MESH = pl.DeviceIdType.MESH


def ahead(f, axis):
    if axis == 1:
        return pltpu.roll(f, f.shape[2] - 1, 2)
    return jnp.concatenate([f[1:], pltpu.roll(f[:1], 7, 1)], axis=0)


def behind(f, axis):
    if axis == 1:
        return pltpu.roll(f, 1, 2)
    return jnp.concatenate([pltpu.roll(f[-1:], 1, 1), f[:-1]], axis=0)


def dealt(ref, *at):
    folds = ref.shape[-2] // 8
    return jnp.stack([ref[(*at, pl.ds(j, 8, stride=folds), slice(None))] for j in range(folds)])


def next_h(h, e, e_next):
    e1, e2, e3 = e
    x2 = -e2 if e_next is None else e_next[0] - e2
    x3 = -e3 if e_next is None else e_next[1] - e3
    curl = (
        (ahead(e3, 0) - e3) - (ahead(e2, 1) - e2),
        (ahead(e1, 1) - e1) - x3,
        x2 - (ahead(e1, 0) - e1),
    )
    if h is None:
        return tuple(-v for v in curl)
    return tuple(a - v for a, v in zip(h, curl))


def curl_h(h, h_prev):
    h1, h2, h3 = h
    x2 = h2 if h_prev is None else h2 - h_prev[0]
    x3 = h3 if h_prev is None else h3 - h_prev[1]
    return (
        (h3 - behind(h3, 0)) - (h2 - behind(h2, 1)),
        (h1 - behind(h1, 1)) - x3,
        x2 - (h1 - behind(h1, 0)),
    )


def kernel(n, nsrc, fwd, adj, eps, wave, foot_hbm, out,
           foot, JR, CR, J, C, E, H, HI, EL, EH, send_e, send_h, recv_e, recv_h, c_lo, c_hi, j_lo, j_hi,
           q_lo, q_hi, r_lo, r_hi, b_lo, b_hi, e_lo, e_hi, lo_h, lo_e, hi_e, sig, G, R, T, S, U, RT,
           load_sem, es_sem, er_sem, hs_sem, hr_sem, gs_sem, gr_sem, ss_sem, ts_sem, tr_sem):
    me = lax.axis_index("space")
    src = lax.axis_index("src")
    chips, chip, core = n // 2, me // 2, lax.rem(me, 2)
    sibling = 2 * chip + 1 - core
    low, high = lax.rem(me + n - 1, n), lax.rem(me + 1, n)
    has_low, has_high = me > 0, me < n - 1
    ys = foot.shape[1]

    loads = [
        pltpu.make_async_copy(eps, CR, load_sem.at[0]),
        pltpu.make_async_copy(fwd.at[0], JR.at[0], load_sem.at[1]),
        pltpu.make_async_copy(adj.at[0], JR.at[1], load_sem.at[2]),
        pltpu.make_async_copy(foot_hbm, foot, load_sem.at[3]),
    ]
    for copy in loads:
        copy.start()

    barrier = pltpu.get_barrier_semaphore()
    partners = [sibling, lax.rem(me + n + 2 * core - 1, n)] + [2 * lax.rem(chip + d, chips) + core for d in range(1, chips)]
    for device in partners:
        pl.semaphore_signal(barrier, inc=1, device_id={"space": device}, device_id_type=MESH)
    for d in range(1, nsrc):
        pl.semaphore_signal(barrier, inc=1, device_id={"src": lax.rem(src + d, nsrc)}, device_id_type=MESH)

    omega = 0.25 + 0.05 * wave[0].astype(jnp.float32)
    when = (lax.broadcasted_iota(jnp.int32, (8, 128), 0) + 1).astype(jnp.float32)
    sig[0] = jnp.sin(omega * when)
    sig[1] = jnp.cos(omega * when)

    def remote(a, b, s, r, where):
        return pltpu.make_async_remote_copy(
            src_ref=a, dst_ref=b, send_sem=s, recv_sem=r, device_id=where, device_id_type=MESH)

    def copies(pairs, s, r, where):
        return [remote(a, b, s.at[i], r.at[i], where) for i, (a, b) in enumerate(pairs)]

    e_copies = copies((
        (fwd.at[0, pl.ds(1, 2), 0], j_hi.at[0]), (adj.at[0, pl.ds(1, 2), 0], j_hi.at[1]), (eps.at[0], c_hi),
        (send_e, recv_e), (q_lo, r_hi)), es_sem, er_sem, {"space": low})
    h_copies = copies((
        (fwd.at[0, :, 7], j_lo.at[0]), (adj.at[0, :, 7], j_lo.at[1]), (eps.at[7], c_lo),
        (send_h, recv_h), (q_hi, r_lo)), hs_sem, hr_sem, {"space": high})

    def start_e(*those):
        pl.when(has_low)(lambda: [e_copies[i].start() for i in those] and None)

    def start_h(*those):
        pl.when(has_high)(lambda: [h_copies[i].start() for i in those] and None)

    def arrived(*those):
        pl.when(has_low)(lambda: [h_copies[i].wait_recv() for i in those] and None)
        pl.when(has_high)(lambda: [e_copies[i].wait_recv() for i in those] and None)

    @pl.when(jnp.logical_not(has_low))
    def _():
        for ref in (recv_h, c_lo, j_lo, r_lo):
            ref[...] = jnp.zeros_like(ref)

    @pl.when(jnp.logical_not(has_high))
    def _():
        for ref in (recv_e, c_hi, j_hi, r_hi):
            ref[...] = jnp.zeros_like(ref)

    m_lo = jnp.where(has_low, 1.0, 0.0).astype(jnp.float32)
    m_hi = jnp.where(has_high, 1.0, 0.0).astype(jnp.float32)

    def get(ref, *at):
        return tuple(ref[(*at[:-1], k, at[-1])] for k in range(3))

    def put(ref, vals, *at):
        for k in range(3):
            ref[(*at[:-1], k, at[-1])] = vals[k]

    def get3(ref, r):
        return tuple(ref[r, k] for k in range(3))

    def put3(ref, r, vals):
        for k in range(3):
            ref[r, k] = vals[k]

    def pair(ref, r):
        return ref[r, 0], ref[r, 1]

    def put_pair(ref, r, vals):
        ref[r, 0], ref[r, 1] = vals[1], vals[2]

    def e_at(t, r, p):
        return tuple(E[t, r, k, p] for k in range(3))

    def step_e(t, r, p, e, h, h_prev):
        c, s = C[p], sig[r, t:t + 1, :]
        curl = curl_h(h, h_prev)
        return tuple(e[k] + c * curl[k] - s * J[r, k, p] for k in range(3))

    def h_at(r, p):
        return tuple(H[r, k, p] for k in range(3))

    def new_h(t, r, p):
        return next_h(None if t == 0 else h_at(r, p), e_at(t, r, p), (E[t, r, 1, p + 1], E[t, r, 2, p + 1]))

    def put_e(t, r, p, new):
        for k in range(3):
            E[t, r, k, p] = new[k]

    def runs(body):
        lax.fori_loop(0, 2, lambda r, _: (body(r), 0)[1], 0)

    def planes(first, last, body):
        lax.fori_loop(first, last, lambda p, _: (body(p), 0)[1], 0)

    folds = C.shape[1]
    CHUNK = 2

    def rows(ref, at, first, count):
        if first < 0:
            return jnp.concatenate([pltpu.roll(ref[(*at, pl.ds(folds - 1, 1))], 1, 1), ref[(*at, pl.ds(0, count - 1))]], axis=0)
        if first + count > folds:
            return jnp.concatenate([ref[(*at, pl.ds(first, count - 1))], pltpu.roll(ref[(*at, pl.ds(0, 1))], 7, 1)], axis=0)
        return ref[(*at, pl.ds(first, count))]

    def sweep_h(t, r, p):
        for j in range(0, folds, CHUNK):
            here = pl.ds(j, CHUNK)
            e1, e2, e3 = (E[t, r, k, p, here] for k in range(3))
            d1 = (rows(E, (t, r, 2, p), j + 1, CHUNK) - e3) - (ahead(e2, 1) - e2)
            d2 = (ahead(e1, 1) - e1) - (E[t, r, 2, p + 1, here] - e3)
            d3 = (E[t, r, 1, p + 1, here] - e2) - (rows(E, (t, r, 0, p), j + 1, CHUNK) - e1)
            for k, d in enumerate((d1, d2, d3)):
                H[r, k, p, here] = -d if t == 0 else H[r, k, p, here] - d

    def sweep_e(t, r, p):
        s = sig[r, t:t + 1, :]
        for j in range(0, folds, CHUNK):
            here = pl.ds(j, CHUNK)
            c = C[p, here]
            h1, h2, h3 = (H[r, k, p, here] for k in range(3))
            d1 = (h3 - rows(H, (r, 2, p), j - 1, CHUNK)) - (h2 - behind(h2, 1))
            d2 = (h1 - behind(h1, 1)) - (h3 - H[r, 2, p - 1, here])
            d3 = (h2 - H[r, 1, p - 1, here]) - (h1 - rows(H, (r, 0, p), j - 1, CHUNK))
            for k, d in enumerate((d1, d2, d3)):
                E[t, r, k, p, here] = E[t - 1, r, k, p, here] + c * d - s * J[r, k, p, here]

    def sweep(t, first, last):
        for r in range(2):
            sweep_h(t, r, first)

        def body(p):
            for r in range(2):
                sweep_h(t, r, p)
            for r in range(2):
                sweep_e(t + 1, r, p)

        planes(first + 1, last, body)

    def begin(p):
        c = 0.25 * dealt(CR, p)
        for r in range(2):
            s = sig[r, 0:1, :]
            for k in range(3):
                a = 2.0 * c * dealt(JR, r, k, p)
                J[r, k, p] = a
                E[0, r, k, p] = -s * a
        C[p] = c

    pl.semaphore_wait(barrier, chips + 1 + nsrc - 1)
    start_e(0, 1, 2)
    start_h(0, 1, 2)
    for copy in loads:
        copy.wait()

    planes(0, 8, begin)
    sweep(0, 0, 7)

    def alone(r):
        h0, h6, e1, e2, e3 = h_at(r, 0), h_at(r, 6), e_at(0, r, 0), e_at(1, r, 1), e_at(0, r, 7)
        e6 = e_at(1, r, 6)
        h7 = next_h(None, e3, None)
        e7 = step_e(1, r, 7, e3, h7, h6[1:])
        h7 = next_h(h7, e7, None)
        e0 = step_e(1, r, 0, e1, h0, None)
        put_pair(send_e, r, e0)
        put_pair(send_h, r, h7)
        put3(EL, r, step_e(2, r, 0, e0, next_h(h0, e0, e2[1:]), None))
        h6 = next_h(h6, e6, e7[1:])
        put3(HI, r, next_h(h7, step_e(2, r, 7, e7, h7, h6[1:]), None))

    runs(alone)
    start_e(3)
    start_h(3)
    sweep(1, 1, 6)
    sweep(2, 2, 5)

    arrived(0, 1, 2)
    b_lo[...] = 0.25 * dealt(c_lo)
    b_hi[...] = 0.25 * dealt(c_hi)

    def edges(r):
        s = sig[r, 0:1, :]
        for k in range(3):
            e_lo[r, k] = -s * (2.0 * b_lo[...] * dealt(j_lo, r, k))
        for k in range(2):
            e_hi[r, k] = -s * (2.0 * b_hi[...] * dealt(j_hi, r, k))

    runs(edges)
    for_low, for_high = None, None
    for r in range(2):
        curl = curl_h((jnp.zeros_like(EL[r, 0]), EL[r, 2], -EL[r, 1]), None)
        terms = [e_lo[1 - r, k] * curl[k] for k in range(3)]
        term = terms[0] + terms[1] + terms[2]
        for_low = term if for_low is None else for_low + term
        term = e_hi[1 - r, 0] * HI[r, 2] - e_hi[1 - r, 1] * HI[r, 1]
        for_high = term if for_high is None else for_high + term
    q_lo[...] = b_lo[...] * for_low
    q_hi[...] = b_hi[...] * for_high
    start_e(4)
    start_h(4)

    def product(p, more=None):
        total = more
        for t in range(ITERS):
            for k in range(3):
                term = E[t, 0, k, p] * E[ITERS - 1 - t, 1, k, p]
                total = term if total is None else total + term
        folds = total.shape[0]
        for j in range(folds):
            G[p, pl.ds(j, 8, stride=folds), :] = total[j]

    def share(j):
        return pl.ds(pl.multiple_of(j * ys, 8), ys)

    g_copies = []
    for piece, (start, size) in enumerate(PIECES):
        g_copies.append([
            remote(G.at[pl.ds(start, size), share(lax.rem(src + d, nsrc))], R.at[d - 1, pl.ds(start, size)],
                   gs_sem.at[d - 1, piece], gr_sem.at[d - 1, piece], {"src": lax.rem(src + d, nsrc)})
            for d in range(1, nsrc)
        ])

    def start_g(piece):
        for copy in g_copies[piece]:
            copy.start()

    def step2(r):
        e0, e7, h0, h1, h5, h6 = e_at(0, r, 0), e_at(0, r, 7), h_at(r, 0), h_at(r, 1), h_at(r, 5), h_at(r, 6)
        e1, e6, f2, f5 = e_at(1, r, 1), e_at(1, r, 6), e_at(2, r, 2), e_at(2, r, 5)
        d2, d3 = m_lo * e0[2], -m_lo * e0[1]
        zero = jnp.zeros_like(d2)
        h = next_h(None, get3(e_lo, r), None)
        e0 = step_e(1, r, 0, e0, h0, (h[1] + d2, h[2] + d3))
        de = tuple(b_lo[...] * v for v in curl_h((zero, d2, d3), None))
        h0 = next_h(h0, e0, e1[1:])
        f1 = step_e(2, r, 1, e1, h1, h0[1:])
        h1 = next_h(h1, f1, f2[1:])
        g2 = step_e(3, r, 2, f2, h_at(r, 2), h1[1:])
        h7 = next_h(None, e7, pair(e_hi, r))
        e7 = step_e(1, r, 7, e7, h7, h6[1:])
        c = m_hi * b_hi[...]
        h6 = next_h(h6, e6, e7[1:])
        f6 = step_e(2, r, 6, e6, h6, h5[1:])
        h5 = next_h(h5, f5, f6[1:])
        g5 = step_e(3, r, 5, f5, h5, (H[r, 1, 4], H[r, 2, 4]))
        put3(lo_h, r, (zero, d2, d3))
        put3(lo_e, r, de)
        put3(hi_e, r, (zero, c * h7[2], -c * h7[1]))
        for p, h in ((0, h0), (1, h1), (5, h5), (6, h6), (7, h7)):
            put(H, h, r, p)
        for t, p, e in ((1, 0, e0), (2, 1, f1), (3, 2, g2), (1, 7, e7), (2, 6, f6), (3, 5, g5)):
            put_e(t, r, p, e)

    runs(step2)
    lax.fori_loop(2, 6, lambda p, _: (product(p), 0)[1], 0)
    start_g(0)
    arrived(3)

    def step3(r):
        e0, e7, f1, f6 = e_at(1, r, 0), e_at(1, r, 7), e_at(2, r, 1), e_at(2, r, 6)
        h0, h6, h7 = h_at(r, 0), h_at(r, 6), h_at(r, 7)
        de, dh = get3(lo_e, r), get3(lo_h, r)
        dh = next_h(dh, de, (m_lo * e0[1], m_lo * e0[2]))
        h = pair(recv_h, r)
        f0 = step_e(2, r, 0, e0, h0, (h[0] + dh[1], h[1] + dh[2]))
        curl = curl_h(dh, (de[2], -de[1]))
        de = tuple(de[k] + b_lo[...] * curl[k] for k in range(3))
        dh = next_h(dh, de, (m_lo * f0[1], m_lo * f0[2]))
        h0 = next_h(h0, f0, f1[1:])
        g0 = step_e(3, r, 0, f0, h0, dh[1:])
        g1 = step_e(3, r, 1, f1, h_at(r, 1), h0[1:])
        de, e = get3(hi_e, r), pair(recv_e, r)
        h7 = next_h(h7, e7, (e[0] + de[1], e[1] + de[2]))
        f7 = step_e(2, r, 7, e7, h7, h6[1:])
        curl = curl_h(next_h(None, de, None), (m_hi * h7[1], m_hi * h7[2]))
        de = tuple(de[k] + b_hi[...] * curl[k] for k in range(3))
        h7 = next_h(h7, f7, de[1:])
        h6 = next_h(h6, f6, f7[1:])
        g7 = step_e(3, r, 7, f7, h7, h6[1:])
        g6 = step_e(3, r, 6, f6, h6, (H[r, 1, 5], H[r, 2, 5]))
        for t, p, e in ((2, 0, f0), (3, 0, g0), (3, 1, g1), (2, 7, f7), (3, 7, g7), (3, 6, g6)):
            put_e(t, r, p, e)

    runs(step3)
    product(1)
    start_g(1)
    product(6)
    start_g(2)
    arrived(4)
    product(0, r_lo[...])
    start_g(3)
    product(7, r_hi[...])
    start_g(4)

    pixels = n * PIX_DEV
    ids = foot[...] - src * pixels
    total = None
    for pieces in ((0,), (1, 2), (3, 4)):
        heads, tails, chosen = [], [], []
        for piece in pieces:
            for copy in g_copies[piece]:
                copy.wait_recv()
            start, size = PIECES[piece]
            for p in range(start, start + size):
                block = G[p, share(src), :]
                for d in range(1, nsrc):
                    block = block + R[d - 1, p]
                head = block.astype(jnp.bfloat16).astype(jnp.float32)
                heads.append(head)
                tails.append(block - head)
                chosen.append(ids[p:p + 1, :])
        row = lax.broadcasted_iota(jnp.int32, (pixels, len(chosen) * ys), 0)
        select = (row == jnp.concatenate(chosen, axis=1)).astype(jnp.float32).astype(jnp.bfloat16)
        for part in (heads, tails):
            part = jnp.concatenate(part, axis=0).astype(jnp.bfloat16)
            term = jnp.dot(select, part, preferred_element_type=jnp.float32)
            total = term if total is None else total + term
    for owner in range(n):
        T[owner % 2, owner // 2] = total[owner * PIX_DEV:(owner + 1) * PIX_DEV]
    swap = remote(T.at[1 - core], S, ss_sem.at[0], ss_sem.at[1], {"space": sibling})
    swap.start()
    swap.wait_recv()
    U[...] = T[core] + S[...]

    t_copies = [
        remote(U.at[lax.rem(chip + d, chips)], RT.at[d - 1], ts_sem.at[d - 1], tr_sem.at[d - 1],
               {"space": 2 * lax.rem(chip + d, chips) + core})
        for d in range(1, chips)
    ]
    for copy in t_copies:
        copy.start()
    result = U[chip]
    for d in range(1, chips):
        t_copies[d - 1].wait_recv()
        result = result + RT[d - 1]
    out[...] = result

    swap.wait_send()
    for copy in t_copies:
        copy.wait_send()
    for piece in g_copies:
        for copy in piece:
            copy.wait_send()
    pl.when(has_low)(lambda: [copy.wait_send() for copy in e_copies] and None)
    pl.when(has_high)(lambda: [copy.wait_send() for copy in h_copies] and None)


def solution(mesh):
    n, nsrc = mesh.shape["space"], mesh.shape["src"]

    def per_device(fwd, adj, eps, wave, foot):
        cx, ny, nz = eps.shape
        ys = foot.shape[1]
        f32 = jnp.float32
        raw, plane = (ny, nz), (ny // 8, 8, nz)

        def vmem(*shape):
            return pltpu.VMEM(shape, f32)

        dma = pltpu.SemaphoreType.DMA
        hbm = pl.BlockSpec(memory_space=pltpu.HBM)
        return pl.pallas_call(
            functools.partial(kernel, n, nsrc),
            out_shape=jax.ShapeDtypeStruct((PIX_DEV, nz), f32),
            in_specs=[hbm, hbm, hbm, pl.BlockSpec(memory_space=pltpu.SMEM), hbm],
            out_specs=pl.BlockSpec(memory_space=pltpu.VMEM),
            scratch_shapes=[
                pltpu.VMEM(foot.shape, jnp.int32), vmem(2, 3, cx, *raw), vmem(cx, *raw),
                vmem(2, 3, cx, *plane), vmem(cx, *plane), vmem(ITERS, 2, 3, cx, *plane),
                vmem(2, 3, cx, *plane), vmem(2, 3, *plane), vmem(2, 3, *plane), vmem(2, 3, *plane),
                vmem(2, 2, *plane), vmem(2, 2, *plane), vmem(2, 2, *plane), vmem(2, 2, *plane),
                vmem(*raw), vmem(*raw), vmem(2, 3, *raw), vmem(2, 2, *raw),
                vmem(*plane), vmem(*plane), vmem(*plane), vmem(*plane), vmem(*plane), vmem(*plane),
                vmem(2, 3, *plane), vmem(2, 2, *plane),
                vmem(2, 3, *plane), vmem(2, 3, *plane), vmem(2, 3, *plane), vmem(2, 8, 128),
                vmem(cx, *raw), vmem(nsrc - 1, cx, ys, nz),
                vmem(2, n // 2, PIX_DEV, nz), vmem(n // 2, PIX_DEV, nz), vmem(n // 2, PIX_DEV, nz),
                vmem(n // 2 - 1, PIX_DEV, nz),
                dma((4,)), dma((5,)), dma((5,)), dma((5,)), dma((5,)),
                dma((nsrc - 1, len(PIECES))), dma((nsrc - 1, len(PIECES))), dma((2,)), dma((n // 2 - 1,)), dma((n // 2 - 1,)),
            ],
            compiler_params=pltpu.CompilerParams(
                collective_id=0, has_side_effects=True, vmem_limit_bytes=60 * 1024 * 1024),
            cost_estimate=pl.CostEstimate(flops=30_000_000, bytes_accessed=2_000_000, transcendentals=0),
        )(fwd, adj, eps, wave, foot)

    in_specs = (
        P("src", None, "space", None, None),
        P("src", None, "space", None, None),
        P("space", None, None),
        P("src"),
        P("space", "src"),
    )
    return jax.shard_map(
        per_device, mesh=mesh, in_specs=in_specs, out_specs=P(("src", "space"), None), check_vma=False)
```

```python
import functools

import jax
import jax.numpy as jnp
from jax import lax
from jax.experimental import pallas as pl
from jax.experimental.pallas import tpu as pltpu
from jax.sharding import PartitionSpec as P

ITERS = 4
PIX_DEV = 16
PIECES = ((2, 4), (0, 2), (6, 2))
MESH = pl.DeviceIdType.MESH


def ahead(f, axis):
    if axis == 1:
        return pltpu.roll(f, f.shape[2] - 1, 2)
    return jnp.concatenate([f[1:], pltpu.roll(f[:1], 7, 1)], axis=0)


def behind(f, axis):
    if axis == 1:
        return pltpu.roll(f, 1, 2)
    return jnp.concatenate([pltpu.roll(f[-1:], 1, 1), f[:-1]], axis=0)


def dealt(ref, *at):
    folds = ref.shape[-2] // 8
    return jnp.stack([ref[(*at, pl.ds(j, 8, stride=folds), slice(None))] for j in range(folds)])


def next_h(h, e, e_next):
    e1, e2, e3 = e
    x2 = -e2 if e_next is None else e_next[0] - e2
    x3 = -e3 if e_next is None else e_next[1] - e3
    curl = (
        (ahead(e3, 0) - e3) - (ahead(e2, 1) - e2),
        (ahead(e1, 1) - e1) - x3,
        x2 - (ahead(e1, 0) - e1),
    )
    if h is None:
        return tuple(-v for v in curl)
    return tuple(a - v for a, v in zip(h, curl))


def curl_h(h, h_prev):
    h1, h2, h3 = h
    x2 = h2 if h_prev is None else h2 - h_prev[0]
    x3 = h3 if h_prev is None else h3 - h_prev[1]
    return (
        (h3 - behind(h3, 0)) - (h2 - behind(h2, 1)),
        (h1 - behind(h1, 1)) - x3,
        x2 - (h1 - behind(h1, 0)),
    )


def kernel(n, nsrc, fwd, adj, eps, wave, foot_hbm, out,
           foot, JR, CR, J, C, E, H, HI, EL, EH, send_e, send_h, recv_e, recv_h, c_lo, c_hi, j_lo, j_hi,
           q_lo, q_hi, r_lo, r_hi, b_lo, b_hi, e_lo, e_hi, lo_h, lo_e, hi_e, sig, G, R, T, S, U, RT,
           load_sem, es_sem, er_sem, hs_sem, hr_sem, gs_sem, gr_sem, ss_sem, ts_sem, tr_sem):
    me = lax.axis_index("space")
    src = lax.axis_index("src")
    chips, chip, core = n // 2, me // 2, lax.rem(me, 2)
    sibling = 2 * chip + 1 - core
    low, high = lax.rem(me + n - 1, n), lax.rem(me + 1, n)
    has_low, has_high = me > 0, me < n - 1
    ys = foot.shape[1]

    loads = [
        pltpu.make_async_copy(eps, CR, load_sem.at[0]),
        pltpu.make_async_copy(fwd.at[0], JR.at[0], load_sem.at[1]),
        pltpu.make_async_copy(adj.at[0], JR.at[1], load_sem.at[2]),
        pltpu.make_async_copy(foot_hbm, foot, load_sem.at[3]),
    ]
    for copy in loads:
        copy.start()

    barrier = pltpu.get_barrier_semaphore()
    partners = [sibling, lax.rem(me + n + 2 * core - 1, n)] + [2 * lax.rem(chip + d, chips) + core for d in range(1, chips)]
    for device in partners:
        pl.semaphore_signal(barrier, inc=1, device_id={"space": device}, device_id_type=MESH)
    for d in range(1, nsrc):
        pl.semaphore_signal(barrier, inc=1, device_id={"src": lax.rem(src + d, nsrc)}, device_id_type=MESH)

    omega = 0.25 + 0.05 * wave[0].astype(jnp.float32)
    when = (lax.broadcasted_iota(jnp.int32, (8, 128), 0) + 1).astype(jnp.float32)
    sig[0] = jnp.sin(omega * when)
    sig[1] = jnp.cos(omega * when)

    def remote(a, b, s, r, where):
        return pltpu.make_async_remote_copy(
            src_ref=a, dst_ref=b, send_sem=s, recv_sem=r, device_id=where, device_id_type=MESH)

    def copies(pairs, s, r, where):
        return [remote(a, b, s.at[i], r.at[i], where) for i, (a, b) in enumerate(pairs)]

    e_copies = copies((
        (fwd.at[0, pl.ds(1, 2), 0], j_hi.at[0]), (adj.at[0, pl.ds(1, 2), 0], j_hi.at[1]), (eps.at[0], c_hi),
        (send_e, recv_e), (q_lo, r_hi)), es_sem, er_sem, {"space": low})
    h_copies = copies((
        (fwd.at[0, :, 7], j_lo.at[0]), (adj.at[0, :, 7], j_lo.at[1]), (eps.at[7], c_lo),
        (send_h, recv_h), (q_hi, r_lo)), hs_sem, hr_sem, {"space": high})

    def start_e(*those):
        pl.when(has_low)(lambda: [e_copies[i].start() for i in those] and None)

    def start_h(*those):
        pl.when(has_high)(lambda: [h_copies[i].start() for i in those] and None)

    def arrived(*those):
        pl.when(has_low)(lambda: [h_copies[i].wait_recv() for i in those] and None)
        pl.when(has_high)(lambda: [e_copies[i].wait_recv() for i in those] and None)

    @pl.when(jnp.logical_not(has_low))
    def _():
        for ref in (recv_h, c_lo, j_lo, r_lo):
            ref[...] = jnp.zeros_like(ref)

    @pl.when(jnp.logical_not(has_high))
    def _():
        for ref in (recv_e, c_hi, j_hi, r_hi):
            ref[...] = jnp.zeros_like(ref)

    m_lo = jnp.where(has_low, 1.0, 0.0).astype(jnp.float32)
    m_hi = jnp.where(has_high, 1.0, 0.0).astype(jnp.float32)

    def get(ref, *at):
        return tuple(ref[(*at[:-1], k, at[-1])] for k in range(3))

    def put(ref, vals, *at):
        for k in range(3):
            ref[(*at[:-1], k, at[-1])] = vals[k]

    def get3(ref, r):
        return tuple(ref[r, k] for k in range(3))

    def put3(ref, r, vals):
        for k in range(3):
            ref[r, k] = vals[k]

    def pair(ref, r):
        return ref[r, 0], ref[r, 1]

    def put_pair(ref, r, vals):
        ref[r, 0], ref[r, 1] = vals[1], vals[2]

    def e_at(t, r, p):
        return tuple(E[t, r, k, p] for k in range(3))

    def step_e(t, r, p, e, h, h_prev):
        c, s = C[p], sig[r, t:t + 1, :]
        curl = curl_h(h, h_prev)
        return tuple(e[k] + c * curl[k] - s * J[r, k, p] for k in range(3))

    def h_at(r, p):
        return tuple(H[r, k, p] for k in range(3))

    def new_h(t, r, p):
        return next_h(None if t == 0 else h_at(r, p), e_at(t, r, p), (E[t, r, 1, p + 1], E[t, r, 2, p + 1]))

    def put_e(t, r, p, new):
        for k in range(3):
            E[t, r, k, p] = new[k]

    def runs(body):
        lax.fori_loop(0, 2, lambda r, _: (body(r), 0)[1], 0)

    def planes(first, last, body):
        lax.fori_loop(first, last, lambda p, _: (body(p), 0)[1], 0)

    def sweep(t, first, last):
        hs = [new_h(t, r, first) for r in range(2)]
        for r in range(2):
            put(H, hs[r], r, first)

        def body(p):
            hs = [new_h(t, r, p) for r in range(2)]
            es = [step_e(t + 1, r, p, e_at(t, r, p), hs[r], (H[r, 1, p - 1], H[r, 2, p - 1])) for r in range(2)]
            for r in range(2):
                put(H, hs[r], r, p)
                put_e(t + 1, r, p, es[r])

        planes(first + 1, last, body)

    def begin(p):
        c = 0.25 * dealt(CR, p)
        for r in range(2):
            s = sig[r, 0:1, :]
            for k in range(3):
                a = 2.0 * c * dealt(JR, r, k, p)
                J[r, k, p] = a
                E[0, r, k, p] = -s * a
        C[p] = c

    pl.semaphore_wait(barrier, chips + 1 + nsrc - 1)
    start_e(0, 1, 2)
    start_h(0, 1, 2)
    for copy in loads:
        copy.wait()

    planes(0, 8, begin)
    sweep(0, 0, 7)

    def alone(r):
        h0, h6, e1, e2, e3 = h_at(r, 0), h_at(r, 6), e_at(0, r, 0), e_at(1, r, 1), e_at(0, r, 7)
        e6 = e_at(1, r, 6)
        h7 = next_h(None, e3, None)
        e7 = step_e(1, r, 7, e3, h7, h6[1:])
        h7 = next_h(h7, e7, None)
        e0 = step_e(1, r, 0, e1, h0, None)
        put_pair(send_e, r, e0)
        put_pair(send_h, r, h7)
        put3(EL, r, step_e(2, r, 0, e0, next_h(h0, e0, e2[1:]), None))
        h6 = next_h(h6, e6, e7[1:])
        put3(HI, r, next_h(h7, step_e(2, r, 7, e7, h7, h6[1:]), None))

    runs(alone)
    start_e(3)
    start_h(3)
    sweep(1, 1, 6)
    sweep(2, 2, 5)

    def product(p, more=None):
        total = more
        for t in range(ITERS):
            for k in range(3):
                term = E[t, 0, k, p] * E[ITERS - 1 - t, 1, k, p]
                total = term if total is None else total + term
        folds = total.shape[0]
        for j in range(folds):
            G[p, pl.ds(j, 8, stride=folds), :] = total[j]

    lax.fori_loop(3, 5, lambda p, _: (product(p), 0)[1], 0)

    arrived(0, 1, 2)
    b_lo[...] = 0.25 * dealt(c_lo)
    b_hi[...] = 0.25 * dealt(c_hi)

    def edges(r):
        s = sig[r, 0:1, :]
        for k in range(3):
            e_lo[r, k] = -s * (2.0 * b_lo[...] * dealt(j_lo, r, k))
        for k in range(2):
            e_hi[r, k] = -s * (2.0 * b_hi[...] * dealt(j_hi, r, k))

    runs(edges)
    for_low, for_high = None, None
    for r in range(2):
        curl = curl_h((jnp.zeros_like(EL[r, 0]), EL[r, 2], -EL[r, 1]), None)
        terms = [e_lo[1 - r, k] * curl[k] for k in range(3)]
        term = terms[0] + terms[1] + terms[2]
        for_low = term if for_low is None else for_low + term
        term = e_hi[1 - r, 0] * HI[r, 2] - e_hi[1 - r, 1] * HI[r, 1]
        for_high = term if for_high is None else for_high + term
    q_lo[...] = b_lo[...] * for_low
    q_hi[...] = b_hi[...] * for_high
    start_e(4)
    start_h(4)

    def share(j):
        return pl.ds(pl.multiple_of(j * ys, 8), ys)

    g_copies = []
    for piece, (start, size) in enumerate(PIECES):
        g_copies.append([
            remote(G.at[pl.ds(start, size), share(lax.rem(src + d, nsrc))], R.at[d - 1, pl.ds(start, size)],
                   gs_sem.at[d - 1, piece], gr_sem.at[d - 1, piece], {"src": lax.rem(src + d, nsrc)})
            for d in range(1, nsrc)
        ])

    def start_g(piece):
        for copy in g_copies[piece]:
            copy.start()

    def step2(r):
        e0, e7, h0, h1, h5, h6 = e_at(0, r, 0), e_at(0, r, 7), h_at(r, 0), h_at(r, 1), h_at(r, 5), h_at(r, 6)
        e1, e6, f2, f5 = e_at(1, r, 1), e_at(1, r, 6), e_at(2, r, 2), e_at(2, r, 5)
        d2, d3 = m_lo * e0[2], -m_lo * e0[1]
        zero = jnp.zeros_like(d2)
        h = next_h(None, get3(e_lo, r), None)
        e0 = step_e(1, r, 0, e0, h0, (h[1] + d2, h[2] + d3))
        de = tuple(b_lo[...] * v for v in curl_h((zero, d2, d3), None))
        h0 = next_h(h0, e0, e1[1:])
        f1 = step_e(2, r, 1, e1, h1, h0[1:])
        h1 = next_h(h1, f1, f2[1:])
        g2 = step_e(3, r, 2, f2, h_at(r, 2), h1[1:])
        h7 = next_h(None, e7, pair(e_hi, r))
        e7 = step_e(1, r, 7, e7, h7, h6[1:])
        c = m_hi * b_hi[...]
        h6 = next_h(h6, e6, e7[1:])
        f6 = step_e(2, r, 6, e6, h6, h5[1:])
        h5 = next_h(h5, f5, f6[1:])
        g5 = step_e(3, r, 5, f5, h5, (H[r, 1, 4], H[r, 2, 4]))
        put3(lo_h, r, (zero, d2, d3))
        put3(lo_e, r, de)
        put3(hi_e, r, (zero, c * h7[2], -c * h7[1]))
        for p, h in ((0, h0), (1, h1), (5, h5), (6, h6), (7, h7)):
            put(H, h, r, p)
        for t, p, e in ((1, 0, e0), (2, 1, f1), (3, 2, g2), (1, 7, e7), (2, 6, f6), (3, 5, g5)):
            put_e(t, r, p, e)

    runs(step2)
    lax.fori_loop(0, 2, lambda i, _: (product(2 + 3 * i), 0)[1], 0)
    start_g(0)
    arrived(3)

    def step3(r):
        e0, e7, f1, f6 = e_at(1, r, 0), e_at(1, r, 7), e_at(2, r, 1), e_at(2, r, 6)
        h0, h6, h7 = h_at(r, 0), h_at(r, 6), h_at(r, 7)
        de, dh = get3(lo_e, r), get3(lo_h, r)
        dh = next_h(dh, de, (m_lo * e0[1], m_lo * e0[2]))
        h = pair(recv_h, r)
        f0 = step_e(2, r, 0, e0, h0, (h[0] + dh[1], h[1] + dh[2]))
        curl = curl_h(dh, (de[2], -de[1]))
        de = tuple(de[k] + b_lo[...] * curl[k] for k in range(3))
        dh = next_h(dh, de, (m_lo * f0[1], m_lo * f0[2]))
        h0 = next_h(h0, f0, f1[1:])
        g0 = step_e(3, r, 0, f0, h0, dh[1:])
        g1 = step_e(3, r, 1, f1, h_at(r, 1), h0[1:])
        de, e = get3(hi_e, r), pair(recv_e, r)
        h7 = next_h(h7, e7, (e[0] + de[1], e[1] + de[2]))
        f7 = step_e(2, r, 7, e7, h7, h6[1:])
        curl = curl_h(next_h(None, de, None), (m_hi * h7[1], m_hi * h7[2]))
        de = tuple(de[k] + b_hi[...] * curl[k] for k in range(3))
        h7 = next_h(h7, f7, de[1:])
        h6 = next_h(h6, f6, f7[1:])
        g7 = step_e(3, r, 7, f7, h7, h6[1:])
        g6 = step_e(3, r, 6, f6, h6, (H[r, 1, 5], H[r, 2, 5]))
        for t, p, e in ((2, 0, f0), (3, 0, g0), (3, 1, g1), (2, 7, f7), (3, 7, g7), (3, 6, g6)):
            put_e(t, r, p, e)

    runs(step3)
    product(1)
    product(6)
    arrived(4)
    product(0, r_lo[...])
    start_g(1)
    product(7, r_hi[...])
    start_g(2)

    pixels = n * PIX_DEV
    ids = foot[...] - src * pixels
    total = None
    for pieces in ((0,), (1, 2)):
        heads, tails, chosen = [], [], []
        for piece in pieces:
            for copy in g_copies[piece]:
                copy.wait_recv()
            start, size = PIECES[piece]
            for p in range(start, start + size):
                block = G[p, share(src), :]
                for d in range(1, nsrc):
                    block = block + R[d - 1, p]
                head = block.astype(jnp.bfloat16).astype(jnp.float32)
                heads.append(head)
                tails.append(block - head)
                chosen.append(ids[p:p + 1, :])
        row = lax.broadcasted_iota(jnp.int32, (pixels, len(chosen) * ys), 0)
        select = (row == jnp.concatenate(chosen, axis=1)).astype(jnp.float32).astype(jnp.bfloat16)
        for part in (heads, tails):
            part = jnp.concatenate(part, axis=0).astype(jnp.bfloat16)
            term = jnp.dot(select, part, preferred_element_type=jnp.float32)
            total = term if total is None else total + term
    for owner in range(n):
        T[owner % 2, owner // 2] = total[owner * PIX_DEV:(owner + 1) * PIX_DEV]
    swap = remote(T.at[1 - core], S, ss_sem.at[0], ss_sem.at[1], {"space": sibling})
    swap.start()
    swap.wait_recv()
    U[...] = T[core] + S[...]

    t_copies = [
        remote(U.at[lax.rem(chip + d, chips)], RT.at[d - 1], ts_sem.at[d - 1], tr_sem.at[d - 1],
               {"space": 2 * lax.rem(chip + d, chips) + core})
        for d in range(1, chips)
    ]
    far_first = sorted(range(1, chips), key=lambda d: abs(2 * d - chips))
    for d in far_first:
        t_copies[d - 1].start()
    result = U[chip]
    for d in reversed(far_first):
        t_copies[d - 1].wait_recv()
        result = result + RT[d - 1]
    out[...] = result

    swap.wait_send()
    for copy in t_copies:
        copy.wait_send()
    for piece in g_copies:
        for copy in piece:
            copy.wait_send()
    pl.when(has_low)(lambda: [copy.wait_send() for copy in e_copies] and None)
    pl.when(has_high)(lambda: [copy.wait_send() for copy in h_copies] and None)


def solution(mesh):
    n, nsrc = mesh.shape["space"], mesh.shape["src"]

    def per_device(fwd, adj, eps, wave, foot):
        cx, ny, nz = eps.shape
        ys = foot.shape[1]
        f32 = jnp.float32
        raw, plane = (ny, nz), (ny // 8, 8, nz)

        def vmem(*shape):
            return pltpu.VMEM(shape, f32)

        dma = pltpu.SemaphoreType.DMA
        hbm = pl.BlockSpec(memory_space=pltpu.HBM)
        return pl.pallas_call(
            functools.partial(kernel, n, nsrc),
            out_shape=jax.ShapeDtypeStruct((PIX_DEV, nz), f32),
            in_specs=[hbm, hbm, hbm, pl.BlockSpec(memory_space=pltpu.SMEM), hbm],
            out_specs=pl.BlockSpec(memory_space=pltpu.VMEM),
            scratch_shapes=[
                pltpu.VMEM(foot.shape, jnp.int32), vmem(2, 3, cx, *raw), vmem(cx, *raw),
                vmem(2, 3, cx, *plane), vmem(cx, *plane), vmem(ITERS, 2, 3, cx, *plane),
                vmem(2, 3, cx, *plane), vmem(2, 3, *plane), vmem(2, 3, *plane), vmem(2, 3, *plane),
                vmem(2, 2, *plane), vmem(2, 2, *plane), vmem(2, 2, *plane), vmem(2, 2, *plane),
                vmem(*raw), vmem(*raw), vmem(2, 3, *raw), vmem(2, 2, *raw),
                vmem(*plane), vmem(*plane), vmem(*plane), vmem(*plane), vmem(*plane), vmem(*plane),
                vmem(2, 3, *plane), vmem(2, 2, *plane),
                vmem(2, 3, *plane), vmem(2, 3, *plane), vmem(2, 3, *plane), vmem(2, 8, 128),
                vmem(cx, *raw), vmem(nsrc - 1, cx, ys, nz),
                vmem(2, n // 2, PIX_DEV, nz), vmem(n // 2, PIX_DEV, nz), vmem(n // 2, PIX_DEV, nz),
                vmem(n // 2 - 1, PIX_DEV, nz),
                dma((4,)), dma((5,)), dma((5,)), dma((5,)), dma((5,)),
                dma((nsrc - 1, len(PIECES))), dma((nsrc - 1, len(PIECES))), dma((2,)), dma((n // 2 - 1,)), dma((n // 2 - 1,)),
            ],
            compiler_params=pltpu.CompilerParams(
                collective_id=0, has_side_effects=True, vmem_limit_bytes=60 * 1024 * 1024),
            cost_estimate=pl.CostEstimate(flops=30_000_000, bytes_accessed=2_000_000, transcendentals=0),
        )(fwd, adj, eps, wave, foot)

    in_specs = (
        P("src", None, "space", None, None),
        P("src", None, "space", None, None),
        P("space", None, None),
        P("src"),
        P("space", "src"),
    )
    return jax.shard_map(
        per_device, mesh=mesh, in_specs=in_specs, out_specs=P(("src", "space"), None), check_vma=False)
```
